32 devices in a mesh: seq: 8 (over y, x, core), dp: 4 (over z).
Axes of the slice: x: 2, y: 2, z: 4, core: 2. Of those that a mesh axis runs over, the one named last changes fastest.
Arguments:
- query: bfloat16 [4, 1024, 2048], P('dp', 'seq'), may hold values from -6 to 6
- keys: bfloat16 [4, 1024, 512], P('dp', 'seq'), may hold values from -6 to 6
- values: bfloat16 [4, 1024, 512], P('dp', 'seq'), may hold values from -6 to 6
- out_grad: bfloat16 [4, 1024, 2048], P('dp', 'seq'), may hold values from -16 to 16
- normed_input: bfloat16 [4, 1024, 4096], P('dp', 'seq'), may hold values from -6 to 6
- q_start: int32 [8], P('dp'), may hold values from 256 to 383, as said below
- q_len: int32 [8], P('dp'), may hold values from 1 to 64, as said below
Outputs:
- q_grad: bfloat16 [4, 1024, 2048], P('dp', 'seq')
- k_grad: bfloat16 [4, 1024, 512], P('dp', 'seq')
- v_grad: bfloat16 [4, 1024, 512], P('dp', 'seq')
- kv_weight_grad: float32 [4096, 1024], P(('seq', 'dp'))
The draws below stay inside these ranges and needn't reach their ends.
Inputs may be any that keep to these rules, and one draw needn't show every extreme that they name: `q_start`: the visual part of each sequence ends here. `q_len`: tokens after the question are padding.
All inputs are finite; a program needn't handle non-finite values.
Results may differ from the reference program's by a relative error of at most 0.013.
Values may be sent and summed in bfloat16 or wider, within the bound.
No kernel may reach another device: no remote copies, remote signals or barrier semaphores. Data moves between devices by JAX's collectives and lax.ppermute only.
A program may use at most 128 MiB of HBM per device.

```python
import math
import jax
import jax.numpy as jnp
from jax import lax

D = 4096
HEADS = 16
KV_HEADS = 4
HEAD_DIM = 128
LEN = 512
GROUP = 1024
SEQS = 8
N_DP = 4


def draw_keys(key, part):
    shape_full = (N_DP, GROUP, KV_HEADS, HEAD_DIM)
    base = jnp.clip(jax.random.normal(jax.random.fold_in(key, 21), shape_full, jnp.float32), -6.0, 6.0)
    return base.reshape(N_DP, GROUP, KV_HEADS * HEAD_DIM).astype(jnp.bfloat16)


def draw_query(key, part):
    shape_full = (N_DP, GROUP, HEADS, HEAD_DIM)
    base = jnp.clip(1.5 * jax.random.normal(jax.random.fold_in(key, 31), shape_full, jnp.float32), -6.0, 6.0)
    return base.reshape(N_DP, GROUP, HEADS * HEAD_DIM).astype(jnp.bfloat16)


def draw_q_start(key, part):
    lowest = LEN // 2
    highest = 3 * LEN // 4 - 1
    drawn = jax.random.randint(jax.random.fold_in(key, 11), (SEQS,), lowest, highest + 1)
    order = jax.random.permutation(jax.random.fold_in(key, 12), SEQS)
    drawn = drawn.at[order[0]].set(lowest).at[order[1]].set(highest)
    return drawn.astype(jnp.int32)


def draw_q_len(key, part):
    highest = LEN // 8
    drawn = jax.random.randint(jax.random.fold_in(key, 13), (SEQS,), 1, highest + 1)
    order = jax.random.permutation(jax.random.fold_in(key, 14), SEQS)
    drawn = drawn.at[order[0]].set(1).at[order[1]].set(highest)
    return drawn.astype(jnp.int32)


def with_spikes(result, rng, source, target, parts, factor):
    owner, partner = [(jnp.arange(result.shape[position]) // (result.shape[position] // parts)).reshape([-1 if axis == position else 1 for axis in range(result.ndim)]) for position in (source, target)]
    chosen = jax.random.permutation(rng, parts)[partner]
    strong = (owner == chosen) | (owner == (partner + parts // 2) % parts)
    return jnp.where(strong, factor * result, result)


def steps_of(stream_key, shape, pieces, low, high):
    gain, own = 1.0, jax.random.fold_in(stream_key, 6)
    for position, shards_of in pieces:
        draws = jnp.exp(jax.random.uniform(jax.random.fold_in(own, position), (shards_of,), jnp.float32, low / len(pieces), high / len(pieces)))
        gain = gain * jnp.repeat(draws, shape[position] // shards_of).reshape([-1 if axis == position else 1 for axis in range(len(shape))])
    return gain


def centred(own_key, extent, width, bound, cuts=(), held_as=jnp.bfloat16):
    entries = width * jax.random.normal(own_key, extent, jnp.float32)
    if cuts:
        entries = entries * steps_of(own_key, extent, cuts, -0.22, 0.18)
    return jnp.clip(entries, -bound, bound).astype(held_as)


def heavy_noise(rng, shape, spread, bound, cuts, heavy, held_as=jnp.bfloat16):
    array = spread * jax.random.normal(rng, shape, jnp.float32)
    if cuts:
        array = array * steps_of(rng, shape, cuts, -0.22, 0.18)
    return jnp.clip(with_spikes(array, jax.random.fold_in(rng, 3), *heavy), -bound, bound).astype(held_as)


def setup_inputs(seed: int = 0) -> dict:
    splits = jax.random.split(jax.random.key(seed), 8)
    query = draw_query(jax.random.fold_in(splits[7], 71), 0)
    keys = draw_keys(jax.random.fold_in(splits[7], 71), 0)
    values = centred(splits[2], (N_DP, GROUP, KV_HEADS * HEAD_DIM), 1.0, 6.0, ((0, 4), (1, 8)))
    out_grad = centred(splits[3], (N_DP, GROUP, HEADS * HEAD_DIM), 4.0, 16.0, ((0, 4), (1, 8)))
    normed_input = heavy_noise(splits[4], (N_DP, GROUP, D), 1.0, 6.0, ((0, 4), (1, 8)), (1, 2, 8, 2.0))
    q_start = draw_q_start(jax.random.fold_in(splits[7], 71), 0)
    q_len = draw_q_len(jax.random.fold_in(splits[7], 71), 0)
    return dict(query=query, keys=keys, values=values, out_grad=out_grad, normed_input=normed_input, q_start=q_start, q_len=q_len)


def sequence_grads(query_seq, keys_seq, values_seq, grad_seq, start_pos, span_len):
    score_scale = 1.0 / math.sqrt(HEAD_DIM)
    repeat_by = HEADS // KV_HEADS
    block_rows = min(512, LEN)
    query_heads = query_seq.reshape(LEN, HEADS, HEAD_DIM).astype(jnp.float32)
    grad_heads = grad_seq.reshape(LEN, HEADS, HEAD_DIM).astype(jnp.float32)
    key_heads = jnp.repeat(keys_seq.reshape(LEN, KV_HEADS, HEAD_DIM), repeat_by, axis=1).astype(jnp.float32)
    value_heads = jnp.repeat(values_seq.reshape(LEN, KV_HEADS, HEAD_DIM), repeat_by, axis=1).astype(jnp.float32)
    key_pos = jnp.arange(LEN, dtype=jnp.int32)
    end_pos = start_pos + span_len

    def one_block(carry, block_idx):
        key_acc, value_acc = carry
        first_row = block_idx * block_rows
        query_block = lax.dynamic_slice_in_dim(query_heads, first_row, block_rows, 0)
        grad_block = lax.dynamic_slice_in_dim(grad_heads, first_row, block_rows, 0)
        query_pos = first_row + jnp.arange(block_rows, dtype=jnp.int32)
        visible = (key_pos[None, :] < end_pos) & ((key_pos[None, :] <= query_pos[:, None]) | (key_pos[None, :] < start_pos))
        scores = jnp.einsum('qhd,khd->hqk', query_block, key_heads) * score_scale
        scores = jnp.where(visible[None], scores, -jnp.inf)
        row_max = lax.optimization_barrier(jnp.max(scores, axis=-1, keepdims=True))
        exponent = jnp.where(visible[None], jnp.exp(scores - row_max), 0.0)
        probability = exponent / lax.optimization_barrier(jnp.sum(exponent, axis=-1, keepdims=True))
        prob_low = lax.optimization_barrier(probability.astype(jnp.bfloat16)).astype(jnp.float32)
        dprob = jnp.einsum('qhd,khd->hqk', grad_block, value_heads)
        row_delta = lax.optimization_barrier(jnp.sum(probability * dprob, axis=-1, keepdims=True))
        dscore = lax.optimization_barrier((probability * (dprob - row_delta) * score_scale).astype(jnp.bfloat16)).astype(jnp.float32)
        query_grad = jnp.einsum('hqk,khd->qhd', dscore, key_heads).astype(jnp.bfloat16)
        key_acc = key_acc + jnp.einsum('hqk,qhd->khd', dscore, query_block)
        value_acc = value_acc + jnp.einsum('hqk,qhd->khd', prob_low, grad_block)
        return ((key_acc, value_acc), query_grad)
    zero_state = jnp.zeros((LEN, HEADS, HEAD_DIM), jnp.float32)
    (key_acc, value_acc), query_grads = lax.scan(one_block, (zero_state, zero_state), jnp.arange(LEN // block_rows, dtype=jnp.int32))
    query_grads = query_grads.reshape(LEN, HEADS * HEAD_DIM)
    key_grads = key_acc.reshape(LEN, KV_HEADS, repeat_by, HEAD_DIM).sum(axis=2).astype(jnp.bfloat16).reshape(LEN, KV_HEADS * HEAD_DIM)
    value_grads = value_acc.reshape(LEN, KV_HEADS, repeat_by, HEAD_DIM).sum(axis=2).astype(jnp.bfloat16).reshape(LEN, KV_HEADS * HEAD_DIM)
    return (query_grads, key_grads, value_grads)

def reference(query, keys, values, out_grad, normed_input, q_start, q_len):
    query_all = []
    key_all = []
    value_all = []
    weight_sum = jnp.zeros((D, 2 * KV_HEADS * HEAD_DIM), jnp.float32)
    for group_idx in range(N_DP):
        query_parts = []
        key_parts = []
        value_parts = []
        for seq_idx in range(2):
            lower = seq_idx * LEN
            upper = lower + LEN
            sample = 2 * group_idx + seq_idx
            query_piece, key_piece, value_piece = sequence_grads(query[group_idx, lower:upper], keys[group_idx, lower:upper], values[group_idx, lower:upper], out_grad[group_idx, lower:upper], q_start[sample], q_len[sample])
            query_parts.append(query_piece)
            key_parts.append(key_piece)
            value_parts.append(value_piece)
        key_group = jnp.concatenate(key_parts, axis=0)
        value_group = jnp.concatenate(value_parts, axis=0)
        joined = jnp.concatenate([key_group, value_group], axis=1)
        weight_sum = weight_sum + jnp.dot(normed_input[group_idx].T, joined, preferred_element_type=jnp.float32)
        query_all.append(jnp.concatenate(query_parts, axis=0))
        key_all.append(key_group)
        value_all.append(value_group)
    return (jnp.stack(query_all), jnp.stack(key_all), jnp.stack(value_all), weight_sum)
```

```python
import functools
import math

import jax
import jax.numpy as jnp
from jax import lax
from jax.experimental import pallas as pl
from jax.experimental.pallas import tpu as pltpu
from jax.sharding import PartitionSpec as P

HEADS = 16
KV_HEADS = 4
HEAD_DIM = 128


def local(query, keys, values, out_grad, normed_input, q_start, q_len):
    seq_count = lax.axis_size("seq")
    tokens_dev = query.shape[1]
    repeat_by = HEADS // KV_HEADS
    classes = max(1, seq_count // HEADS)
    heads_dev = HEADS * classes // seq_count
    head_groups = seq_count // classes
    class_tokens = tokens_dev // classes
    seq_len = tokens_dev * seq_count // 2
    group_tokens = tokens_dev * seq_count
    width_dev = heads_dev * HEAD_DIM
    my_class = lax.axis_index("seq") // head_groups
    score_scale = 1.0 / math.sqrt(HEAD_DIM)

    def to_units(array):
        return array.reshape(class_tokens, seq_count, width_dev)

    query_units = to_units(query[0])
    grad_units = to_units(out_grad[0])
    key_wide = jnp.repeat(
        keys[0].reshape(tokens_dev, KV_HEADS, HEAD_DIM), repeat_by, axis=1
    ).reshape(tokens_dev, HEADS * HEAD_DIM)
    value_wide = jnp.repeat(
        values[0].reshape(tokens_dev, KV_HEADS, HEAD_DIM), repeat_by, axis=1
    ).reshape(tokens_dev, HEADS * HEAD_DIM)
    wide_shape = (tokens_dev, classes, head_groups, width_dev)
    key_units = jnp.broadcast_to(
        key_wide.reshape(tokens_dev, 1, head_groups, width_dev), wide_shape
    ).reshape(tokens_dev, seq_count, width_dev)
    value_units = jnp.broadcast_to(
        value_wide.reshape(tokens_dev, 1, head_groups, width_dev), wide_shape
    ).reshape(tokens_dev, seq_count, width_dev)
    query_got, grad_got, key_got, value_got = (
        lax.all_to_all(query_units, "seq", split_axis=1, concat_axis=0, tiled=True),
        lax.all_to_all(grad_units, "seq", split_axis=1, concat_axis=0, tiled=True),
        lax.all_to_all(key_units, "seq", split_axis=1, concat_axis=0, tiled=True),
        lax.all_to_all(value_units, "seq", split_axis=1, concat_axis=0, tiled=True),
    )
    key_rows = key_got.reshape(group_tokens, heads_dev, HEAD_DIM)
    value_rows = value_got.reshape(group_tokens, heads_dev, HEAD_DIM)
    query_rows = query_got.reshape(seq_count * class_tokens, heads_dev, HEAD_DIM)
    grad_rows = grad_got.reshape(seq_count * class_tokens, heads_dev, HEAD_DIM)
    block_rows = min(512, seq_len // classes)
    blocks_seq = seq_len // classes // block_rows
    key_pos = jnp.arange(seq_len, dtype=jnp.int32)

    def one_block(block_idx, carry):
        query_acc, key_acc, value_acc = carry
        seq_idx = block_idx // blocks_seq
        first_row = block_idx * block_rows
        key_first = seq_idx * seq_len
        query_block = lax.dynamic_slice_in_dim(query_rows, first_row, block_rows, 0)
        grad_block = lax.dynamic_slice_in_dim(grad_rows, first_row, block_rows, 0)
        key_block = lax.dynamic_slice_in_dim(key_rows, key_first, seq_len, 0)
        value_block = lax.dynamic_slice_in_dim(value_rows, key_first, seq_len, 0)
        start_pos = lax.dynamic_index_in_dim(q_start, seq_idx, 0, keepdims=False)
        end_pos = start_pos + lax.dynamic_index_in_dim(q_len, seq_idx, 0, keepdims=False)
        query_pos = (
            (first_row + jnp.arange(block_rows, dtype=jnp.int32)) * classes + my_class - key_first
        )
        visible = (key_pos[None, :] < end_pos) & (
            (key_pos[None, :] <= query_pos[:, None]) | (key_pos[None, :] < start_pos)
        )
        scores = (
            jnp.einsum("qhd,khd->hqk", query_block, key_block, preferred_element_type=jnp.float32)
            * score_scale
        )
        scores = jnp.where(visible[None], scores, -jnp.inf)
        row_max = jnp.max(scores, axis=-1, keepdims=True)
        exponent = jnp.where(visible[None], jnp.exp(scores - row_max), 0.0)
        probability = exponent / jnp.sum(exponent, axis=-1, keepdims=True)
        prob_low = probability.astype(jnp.bfloat16)
        dprob = jnp.einsum(
            "qhd,khd->hqk", grad_block, value_block, preferred_element_type=jnp.float32
        )
        row_delta = jnp.sum(probability * dprob, axis=-1, keepdims=True)
        dscore = (probability * (dprob - row_delta) * score_scale).astype(jnp.bfloat16)
        query_grad = jnp.einsum(
            "hqk,khd->qhd", dscore, key_block, preferred_element_type=jnp.float32
        ).astype(jnp.bfloat16)
        query_acc = lax.dynamic_update_slice_in_dim(query_acc, query_grad, first_row, 0)
        key_part = lax.dynamic_slice_in_dim(key_acc, key_first, seq_len, 0) + jnp.einsum(
            "hqk,qhd->khd", dscore, query_block, preferred_element_type=jnp.float32
        )
        value_part = lax.dynamic_slice_in_dim(value_acc, key_first, seq_len, 0) + jnp.einsum(
            "hqk,qhd->khd", prob_low, grad_block, preferred_element_type=jnp.float32
        )
        key_acc = lax.dynamic_update_slice_in_dim(key_acc, key_part, key_first, 0)
        value_acc = lax.dynamic_update_slice_in_dim(value_acc, value_part, key_first, 0)
        return (query_acc, key_acc, value_acc)

    start_state = (
        jnp.zeros((seq_count * class_tokens, heads_dev, HEAD_DIM), jnp.bfloat16),
        jnp.zeros((group_tokens, heads_dev, HEAD_DIM), jnp.float32),
        jnp.zeros((group_tokens, heads_dev, HEAD_DIM), jnp.float32),
    )
    query_acc, key_acc, value_acc = lax.fori_loop(0, 2 * blocks_seq, one_block, start_state)
    query_back = lax.all_to_all(
        query_acc.reshape(seq_count, class_tokens, 1, width_dev),
        "seq",
        split_axis=0,
        concat_axis=2,
        tiled=True,
    )
    query_grad_out = query_back.reshape(tokens_dev, HEADS * HEAD_DIM)
    key_back, value_back = (
        lax.all_to_all(
            key_acc.reshape(seq_count, tokens_dev, 1, width_dev).astype(jnp.bfloat16),
            "seq",
            split_axis=0,
            concat_axis=2,
            tiled=True,
        ).astype(jnp.float32),
        lax.all_to_all(
            value_acc.reshape(seq_count, tokens_dev, 1, width_dev).astype(jnp.bfloat16),
            "seq",
            split_axis=0,
            concat_axis=2,
            tiled=True,
        ).astype(jnp.float32),
    )
    key_grad_out = (
        key_back.reshape(tokens_dev, classes, KV_HEADS, repeat_by, HEAD_DIM)
        .sum(axis=(1, 3))
        .astype(jnp.bfloat16)
        .reshape(tokens_dev, KV_HEADS * HEAD_DIM)
    )
    value_grad_out = (
        value_back.reshape(tokens_dev, classes, KV_HEADS, repeat_by, HEAD_DIM)
        .sum(axis=(1, 3))
        .astype(jnp.bfloat16)
        .reshape(tokens_dev, KV_HEADS * HEAD_DIM)
    )
    joined = jnp.concatenate([key_grad_out, value_grad_out], axis=1)
    hidden_rows = normed_input[0]
    weight_out = lax.psum_scatter(
        jnp.einsum("tr,tc->rc", hidden_rows, joined, preferred_element_type=jnp.float32),
        ("seq", "dp"),
        scatter_dimension=0,
        tiled=True,
    )
    return (query_grad_out[None], key_grad_out[None], value_grad_out[None], weight_out)


def swap(array, axis, bit):
    size = lax.axis_size(axis)
    return lax.ppermute(array, axis, [(i, i ^ bit) for i in range(size)])


def dot(left, right, dims):
    return lax.dot_general(left, right, (dims, ((), ())), preferred_element_type=jnp.float32)


def lanes(start, width):
    return pl.ds(pl.multiple_of(start, 128), width)


def call(body, outs, args, scratch=(), smem=0, flops=0, vmem=40):
    specs = [pl.BlockSpec(memory_space=pltpu.VMEM)] * (len(args) - smem)
    specs += [pl.BlockSpec(memory_space=pltpu.SMEM)] * smem
    shapes = [jax.ShapeDtypeStruct(shape, dtype) for shape, dtype in outs]
    moved = sum(math.prod(s.shape) * s.dtype.itemsize for s in [*shapes, *args])
    return pl.pallas_call(
        body,
        out_shape=shapes,
        in_specs=specs,
        out_specs=[pl.BlockSpec(memory_space=pltpu.VMEM)] * len(shapes),
        scratch_shapes=list(scratch),
        compiler_params=pltpu.CompilerParams(vmem_limit_bytes=vmem * 2**20),
        cost_estimate=pl.CostEstimate(flops=flops, bytes_accessed=moved, transcendentals=0),
    )(*args)


BF16, F32 = jnp.bfloat16, jnp.float32


def local_pairs(query, keys, values, out_grad, normed_input, q_start, q_len):
    tokens = query.shape[1]
    width = HEADS * HEAD_DIM // 2
    kv_width = KV_HEADS * HEAD_DIM // 2
    own_heads = KV_HEADS // 2
    repeat_by = HEADS // KV_HEADS
    group_width = repeat_by * HEAD_DIM
    seq_len = 4 * tokens
    seen = seq_len * 7 // 8
    model = normed_input.shape[2]
    pair_rows = model // 4
    planes = lax.axis_size("dp")
    part_rows = pair_rows // 2 // planes
    score_scale = 1.0 / math.sqrt(HEAD_DIM)
    query, keys, values, out_grad, hidden = query[0], keys[0], values[0], out_grad[0], normed_input[0]

    def place():
        me = lax.axis_index("seq")
        return me % 2, me % 4, me // 4

    def split_heads(query_ref, grad_ref, key_ref, value_ref, kv_mine, kv_other, send):
        core, _, _ = place()
        for half, kv_out in ((core, kv_mine), (1 - core, kv_other)):
            kv_out[:, :kv_width] = key_ref[:, lanes(half * kv_width, kv_width)]
            kv_out[:, kv_width:] = value_ref[:, lanes(half * kv_width, kv_width)]
        send[:, :width] = query_ref[:, lanes((1 - core) * width, width)]
        send[:, width : 2 * width] = grad_ref[:, lanes((1 - core) * width, width)]
        send[:, 2 * width :] = kv_other[...]

    kv_mine, kv_other, core_send = call(
        split_heads,
        [((tokens, 2 * kv_width), BF16), ((tokens, 2 * kv_width), BF16), ((tokens, 2 * width + 2 * kv_width), BF16)],
        (query, out_grad, keys, values),
    )
    kv_far = swap(kv_mine, "seq", 2)
    kv_cross = swap(kv_other, "seq", 3)
    core_got = swap(core_send, "seq", 1)

    def split_hidden(hidden_ref, *outs):
        pair = lax.axis_index("seq") // 2
        for flip in range(4):
            target = jnp.bitwise_xor(pair, flip)
            outs[flip][...] = hidden_ref[:, lanes(target * pair_rows, pair_rows)]

    hidden_mine, *hidden_send = call(split_hidden, [((tokens, pair_rows), BF16)] * 4, (hidden,))
    hidden_got = [swap(hidden_send[flip - 1], "seq", 2 * flip) for flip in (1, 2, 3)]

    def turn_hidden(mine, far, other, other_far, out):
        half = place()[1] // 2
        for block, (ref, spot) in enumerate(((mine, half), (far, 1 - half), (other, half), (other_far, 1 - half))):
            out[:, lanes((block // 2) * 2 * tokens + spot * tokens, tokens)] = ref[...].T

    (hidden_core,) = call(turn_hidden, [((pair_rows, 4 * tokens), BF16)], (hidden_mine, *hidden_got))
    hidden_pair = swap(hidden_core, "seq", 1)

    def attention(head, query_ref, grad_ref, kv0, got, kv2, kv3, start_ref, len_ref, part, part_low, mine, other, key_all, value_all):
        core, spot, seq_idx = place()
        base = 2 * width
        for flip, ref, offset in ((0, kv0, 0), (1, got, base), (2, kv2, 0), (3, kv3, 0)):
            rows = pl.ds(pl.multiple_of(jnp.bitwise_xor(spot, flip) * tokens, tokens), tokens)
            key_all[rows, :] = ref[:, offset + head * HEAD_DIM : offset + (head + 1) * HEAD_DIM]
            first = offset + kv_width + head * HEAD_DIM
            value_all[rows, :] = ref[:, first : first + HEAD_DIM]
        key = key_all[:seen, :]
        value = value_all[:seen, :]
        start = start_ref[seq_idx]
        end = start + len_ref[seq_idx]
        columns = repeat_by * tokens
        row = lax.broadcasted_iota(jnp.int32, (1, columns), 1) % tokens
        key_pos = lax.broadcasted_iota(jnp.int32, (seen, columns), 0)
        for side, out in enumerate((mine, other)):
            if side == 0:
                blocks = [
                    [ref[:, lanes(core * width + head * group_width + r * HEAD_DIM, HEAD_DIM)] for r in range(repeat_by)]
                    for ref in (query_ref, grad_ref)
                ]
            else:
                blocks = [
                    [got[:, first + r * HEAD_DIM : first + (r + 1) * HEAD_DIM] for r in range(repeat_by)]
                    for first in (head * group_width, width + head * group_width)
                ]
            query_rows = jnp.concatenate(blocks[0], axis=0)
            grad_rows = jnp.concatenate(blocks[1], axis=0)
            query_pos = jnp.bitwise_xor(spot, side) * tokens + row
            limit = jnp.minimum(end, jnp.maximum(start, query_pos + 1))
            scores = dot(key, query_rows, ((1,), (1,)))
            scores = jnp.where(key_pos < limit, scores, -jnp.inf)
            row_max = jnp.max(scores, axis=0, keepdims=True)
            exponent = jnp.exp((scores - row_max) * score_scale)
            probability = exponent * (1.0 / jnp.sum(exponent, axis=0, keepdims=True))
            dprob = dot(value, grad_rows, ((1,), (1,)))
            row_delta = jnp.sum(probability * dprob, axis=0, keepdims=True)
            dscore = (probability * (dprob - row_delta)).astype(BF16)
            key_part = dot(dscore, query_rows, ((1,), (0,))) * score_scale
            value_part = dot(probability.astype(BF16), grad_rows, ((1,), (0,)))
            if side == 0:
                part[:, :HEAD_DIM] = key_part
                part[:, HEAD_DIM:] = value_part
            else:
                part[:, :HEAD_DIM] += key_part
                part[:, HEAD_DIM:] += value_part
            query_grad = dot(key, dscore, ((0,), (0,))) * score_scale
            for r in range(repeat_by):
                out[:, r * HEAD_DIM : (r + 1) * HEAD_DIM] = query_grad[:, r * tokens : (r + 1) * tokens].T.astype(BF16)
        part_low[...] = part[...].astype(BF16)

    def add_parts(part, far, out):
        out[...] = (part[...] + far[...].astype(F32)).astype(BF16)

    def weight(core_ref, pair_ref, own, other, *outs_and_scratch):
        *outs, rows_core, rows_pair = outs_and_scratch
        core, _, _ = place()
        plane = lax.axis_index("dp")
        for seq, ref in enumerate((own, other)):
            padded = jnp.concatenate([ref[...], jnp.zeros((seq_len - seen, 2 * HEAD_DIM), BF16)], axis=0)
            for half in range(2):
                first = jnp.where(core == 0, 0, 1)
                low = padded[2 * half * tokens : (2 * half + 1) * tokens]
                high = padded[(2 * half + 1) * tokens : (2 * half + 2) * tokens]
                spot = (2 * seq + half) * tokens
                rows_core[spot : spot + tokens, :] = jnp.where(first == 0, low, high)
                rows_pair[spot : spot + tokens, :] = jnp.where(first == 0, high, low)
        for flip, out in enumerate(outs):
            target = jnp.bitwise_xor(plane, flip)
            for owner in range(2):
                rows = pl.ds(pl.multiple_of((owner * planes + target) * part_rows, part_rows), part_rows)
                total = dot(core_ref[rows, :], rows_core[...], ((1,), (0,)))
                total += dot(pair_ref[rows, :], rows_pair[...], ((1,), (0,)))
                out[owner * part_rows : (owner + 1) * part_rows, :] = total.astype(out.dtype)

    grads, query_parts, weight_parts = [], [], []
    for head in range(own_heads):
        part, part_low, query_mine, query_other = call(
            functools.partial(attention, head),
            [
                ((seen, 2 * HEAD_DIM), F32),
                ((seen, 2 * HEAD_DIM), BF16),
                ((tokens, group_width), BF16),
                ((tokens, group_width), BF16),
            ],
            (query, out_grad, kv_mine, core_got, kv_far, kv_cross, q_start, q_len),
            scratch=[pltpu.VMEM((seq_len, HEAD_DIM), BF16)] * 2,
            smem=2,
            flops=10 * seen * 2 * group_width * tokens,
        )
        query_parts.append((query_mine, query_other))
        far = swap(part_low, "seq", 2)
        (grad,) = call(add_parts, [((seen, 2 * HEAD_DIM), BF16)], (part, far))
        grads.append(grad)
        grad_other = swap(grad, "seq", 4)
        weight_own, *weight_send = call(
            weight,
            [((2 * part_rows, 2 * HEAD_DIM), F32 if flip == 0 else BF16) for flip in range(planes)],
            (hidden_core, hidden_pair, grad, grad_other),
            scratch=[pltpu.VMEM((4 * tokens, 2 * HEAD_DIM), BF16)] * 2,
            flops=2 * pair_rows * 8 * tokens * 2 * HEAD_DIM,
        )
        weight_parts.append((weight_own, [swap(weight_send[flip - 1], "dp", flip) for flip in range(1, planes)]))

    def pack(grad0, grad1, other0, other1, send, kept):
        _, spot, _ = place()
        for head, (grad, other) in enumerate(((grad0, other0), (grad1, other1))):
            padded = jnp.concatenate([grad[...], jnp.zeros((seq_len - seen, 2 * HEAD_DIM), BF16)], axis=0)
            for ref, wanted in ((kept, spot), (send, jnp.bitwise_xor(spot, 1))):
                chosen = jnp.zeros((tokens, 2 * HEAD_DIM), BF16)
                for block in range(4):
                    chosen = jnp.where(wanted == block, padded[block * tokens : (block + 1) * tokens], chosen)
                ref[:, head * 2 * HEAD_DIM : (head + 1) * 2 * HEAD_DIM] = chosen
            send[:, 2 * kv_width + head * group_width : 2 * kv_width + (head + 1) * group_width] = other[...]

    send, kept = call(
        pack,
        [((tokens, 2 * kv_width + width), BF16), ((tokens, 2 * kv_width), BF16)],
        (*grads, query_parts[0][1], query_parts[1][1]),
    )
    got = swap(send, "seq", 1)

    def unpack(kept_ref, got_ref, mine0, mine1, query_out, key_out, value_out):
        core, _, _ = place()
        for head, mine in enumerate((mine0, mine1)):
            query_out[:, lanes(core * width + head * group_width, group_width)] = mine[...]
            first = 2 * kv_width + head * group_width
            query_out[:, lanes((1 - core) * width + head * group_width, group_width)] = got_ref[:, first : first + group_width]
            for ref, side in ((kept_ref, core), (got_ref, 1 - core)):
                spot = lanes(side * kv_width + head * HEAD_DIM, HEAD_DIM)
                first = head * 2 * HEAD_DIM
                key_out[:, spot] = ref[:, first : first + HEAD_DIM]
                value_out[:, spot] = ref[:, first + HEAD_DIM : first + 2 * HEAD_DIM]

    query_grad, key_grad, value_grad = call(
        unpack,
        [((tokens, 2 * width), BF16), ((tokens, 2 * kv_width), BF16), ((tokens, 2 * kv_width), BF16)],
        (kept, got, query_parts[0][0], query_parts[1][0]),
    )

    def add_planes(own, *refs):
        *got_refs, kept_ref, send_ref = refs
        core, _, _ = place()
        for ref, owner in ((kept_ref, core), (send_ref, 1 - core)):
            rows = pl.ds(pl.multiple_of(owner * part_rows, part_rows), part_rows)
            total = own[rows, :]
            for got_ref in got_refs:
                total += got_ref[rows, :].astype(F32)
            ref[...] = total

    pieces = []
    for weight_own, weight_got in weight_parts:
        kept_weight, send_weight = call(
            add_planes, [((part_rows, 2 * HEAD_DIM), F32)] * 2, (weight_own, *weight_got)
        )
        pieces += [kept_weight, swap(send_weight, "seq", 1)]

    def join(kept0, got0, kept1, got1, out):
        core, _, _ = place()
        for head, (kept_ref, got_ref) in enumerate(((kept0, got0), (kept1, got1))):
            for ref, side in ((kept_ref, core), (got_ref, 1 - core)):
                spot = side * kv_width + head * HEAD_DIM
                out[:, lanes(spot, HEAD_DIM)] = ref[:, :HEAD_DIM]
                out[:, lanes(2 * kv_width + spot, HEAD_DIM)] = ref[:, HEAD_DIM:]

    (weight_grad,) = call(join, [((part_rows, 4 * kv_width), F32)], pieces)
    return query_grad[None], key_grad[None], value_grad[None], weight_grad


def solution(mesh):
    in_specs = (
        P("dp", "seq", None),
        P("dp", "seq", None),
        P("dp", "seq", None),
        P("dp", "seq", None),
        P("dp", "seq", None),
        P("dp"),
        P("dp"),
    )
    out_specs = (
        P("dp", "seq", None),
        P("dp", "seq", None),
        P("dp", "seq", None),
        P(("seq", "dp"), None),
    )
    body = local_pairs if mesh.shape["seq"] == 2 * KV_HEADS else local
    return jax.shard_map(body, mesh=mesh, in_specs=in_specs, out_specs=out_specs, check_vma=False)
```

```python
import functools
import math

import jax
import jax.numpy as jnp
from jax import lax
from jax.experimental import pallas as pl
from jax.experimental.pallas import tpu as pltpu
from jax.sharding import PartitionSpec as P

HEADS = 16
KV_HEADS = 4
HEAD_DIM = 128


def local(query, keys, values, out_grad, normed_input, q_start, q_len):
    seq_count = lax.axis_size("seq")
    tokens_dev = query.shape[1]
    repeat_by = HEADS // KV_HEADS
    classes = max(1, seq_count // HEADS)
    heads_dev = HEADS * classes // seq_count
    head_groups = seq_count // classes
    class_tokens = tokens_dev // classes
    seq_len = tokens_dev * seq_count // 2
    group_tokens = tokens_dev * seq_count
    width_dev = heads_dev * HEAD_DIM
    my_class = lax.axis_index("seq") // head_groups
    score_scale = 1.0 / math.sqrt(HEAD_DIM)

    def to_units(array):
        return array.reshape(class_tokens, seq_count, width_dev)

    query_units = to_units(query[0])
    grad_units = to_units(out_grad[0])
    key_wide = jnp.repeat(
        keys[0].reshape(tokens_dev, KV_HEADS, HEAD_DIM), repeat_by, axis=1
    ).reshape(tokens_dev, HEADS * HEAD_DIM)
    value_wide = jnp.repeat(
        values[0].reshape(tokens_dev, KV_HEADS, HEAD_DIM), repeat_by, axis=1
    ).reshape(tokens_dev, HEADS * HEAD_DIM)
    wide_shape = (tokens_dev, classes, head_groups, width_dev)
    key_units = jnp.broadcast_to(
        key_wide.reshape(tokens_dev, 1, head_groups, width_dev), wide_shape
    ).reshape(tokens_dev, seq_count, width_dev)
    value_units = jnp.broadcast_to(
        value_wide.reshape(tokens_dev, 1, head_groups, width_dev), wide_shape
    ).reshape(tokens_dev, seq_count, width_dev)
    query_got, grad_got, key_got, value_got = (
        lax.all_to_all(query_units, "seq", split_axis=1, concat_axis=0, tiled=True),
        lax.all_to_all(grad_units, "seq", split_axis=1, concat_axis=0, tiled=True),
        lax.all_to_all(key_units, "seq", split_axis=1, concat_axis=0, tiled=True),
        lax.all_to_all(value_units, "seq", split_axis=1, concat_axis=0, tiled=True),
    )
    key_rows = key_got.reshape(group_tokens, heads_dev, HEAD_DIM)
    value_rows = value_got.reshape(group_tokens, heads_dev, HEAD_DIM)
    query_rows = query_got.reshape(seq_count * class_tokens, heads_dev, HEAD_DIM)
    grad_rows = grad_got.reshape(seq_count * class_tokens, heads_dev, HEAD_DIM)
    block_rows = min(512, seq_len // classes)
    blocks_seq = seq_len // classes // block_rows
    key_pos = jnp.arange(seq_len, dtype=jnp.int32)

    def one_block(block_idx, carry):
        query_acc, key_acc, value_acc = carry
        seq_idx = block_idx // blocks_seq
        first_row = block_idx * block_rows
        key_first = seq_idx * seq_len
        query_block = lax.dynamic_slice_in_dim(query_rows, first_row, block_rows, 0)
        grad_block = lax.dynamic_slice_in_dim(grad_rows, first_row, block_rows, 0)
        key_block = lax.dynamic_slice_in_dim(key_rows, key_first, seq_len, 0)
        value_block = lax.dynamic_slice_in_dim(value_rows, key_first, seq_len, 0)
        start_pos = lax.dynamic_index_in_dim(q_start, seq_idx, 0, keepdims=False)
        end_pos = start_pos + lax.dynamic_index_in_dim(q_len, seq_idx, 0, keepdims=False)
        query_pos = (
            (first_row + jnp.arange(block_rows, dtype=jnp.int32)) * classes + my_class - key_first
        )
        visible = (key_pos[None, :] < end_pos) & (
            (key_pos[None, :] <= query_pos[:, None]) | (key_pos[None, :] < start_pos)
        )
        scores = (
            jnp.einsum("qhd,khd->hqk", query_block, key_block, preferred_element_type=jnp.float32)
            * score_scale
        )
        scores = jnp.where(visible[None], scores, -jnp.inf)
        row_max = jnp.max(scores, axis=-1, keepdims=True)
        exponent = jnp.where(visible[None], jnp.exp(scores - row_max), 0.0)
        probability = exponent / jnp.sum(exponent, axis=-1, keepdims=True)
        prob_low = probability.astype(jnp.bfloat16)
        dprob = jnp.einsum(
            "qhd,khd->hqk", grad_block, value_block, preferred_element_type=jnp.float32
        )
        row_delta = jnp.sum(probability * dprob, axis=-1, keepdims=True)
        dscore = (probability * (dprob - row_delta) * score_scale).astype(jnp.bfloat16)
        query_grad = jnp.einsum(
            "hqk,khd->qhd", dscore, key_block, preferred_element_type=jnp.float32
        ).astype(jnp.bfloat16)
        query_acc = lax.dynamic_update_slice_in_dim(query_acc, query_grad, first_row, 0)
        key_part = lax.dynamic_slice_in_dim(key_acc, key_first, seq_len, 0) + jnp.einsum(
            "hqk,qhd->khd", dscore, query_block, preferred_element_type=jnp.float32
        )
        value_part = lax.dynamic_slice_in_dim(value_acc, key_first, seq_len, 0) + jnp.einsum(
            "hqk,qhd->khd", prob_low, grad_block, preferred_element_type=jnp.float32
        )
        key_acc = lax.dynamic_update_slice_in_dim(key_acc, key_part, key_first, 0)
        value_acc = lax.dynamic_update_slice_in_dim(value_acc, value_part, key_first, 0)
        return (query_acc, key_acc, value_acc)

    start_state = (
        jnp.zeros((seq_count * class_tokens, heads_dev, HEAD_DIM), jnp.bfloat16),
        jnp.zeros((group_tokens, heads_dev, HEAD_DIM), jnp.float32),
        jnp.zeros((group_tokens, heads_dev, HEAD_DIM), jnp.float32),
    )
    query_acc, key_acc, value_acc = lax.fori_loop(0, 2 * blocks_seq, one_block, start_state)
    query_back = lax.all_to_all(
        query_acc.reshape(seq_count, class_tokens, 1, width_dev),
        "seq",
        split_axis=0,
        concat_axis=2,
        tiled=True,
    )
    query_grad_out = query_back.reshape(tokens_dev, HEADS * HEAD_DIM)
    key_back, value_back = (
        lax.all_to_all(
            key_acc.reshape(seq_count, tokens_dev, 1, width_dev).astype(jnp.bfloat16),
            "seq",
            split_axis=0,
            concat_axis=2,
            tiled=True,
        ).astype(jnp.float32),
        lax.all_to_all(
            value_acc.reshape(seq_count, tokens_dev, 1, width_dev).astype(jnp.bfloat16),
            "seq",
            split_axis=0,
            concat_axis=2,
            tiled=True,
        ).astype(jnp.float32),
    )
    key_grad_out = (
        key_back.reshape(tokens_dev, classes, KV_HEADS, repeat_by, HEAD_DIM)
        .sum(axis=(1, 3))
        .astype(jnp.bfloat16)
        .reshape(tokens_dev, KV_HEADS * HEAD_DIM)
    )
    value_grad_out = (
        value_back.reshape(tokens_dev, classes, KV_HEADS, repeat_by, HEAD_DIM)
        .sum(axis=(1, 3))
        .astype(jnp.bfloat16)
        .reshape(tokens_dev, KV_HEADS * HEAD_DIM)
    )
    joined = jnp.concatenate([key_grad_out, value_grad_out], axis=1)
    hidden_rows = normed_input[0]
    weight_out = lax.psum_scatter(
        jnp.einsum("tr,tc->rc", hidden_rows, joined, preferred_element_type=jnp.float32),
        ("seq", "dp"),
        scatter_dimension=0,
        tiled=True,
    )
    return (query_grad_out[None], key_grad_out[None], value_grad_out[None], weight_out)


def swap(array, axis, bit):
    size = lax.axis_size(axis)
    return lax.ppermute(array, axis, [(i, i ^ bit) for i in range(size)])


def dot(left, right, dims):
    return lax.dot_general(left, right, (dims, ((), ())), preferred_element_type=jnp.float32)


def lanes(start, width):
    return pl.ds(pl.multiple_of(start, 128), width)


def call(body, outs, args, scratch=(), smem=0, held=0, flops=0, vmem=16, place=pltpu.VMEM):
    near = len(args) - smem - held
    specs = [pl.BlockSpec(memory_space=place)] * near
    specs += [pl.BlockSpec(memory_space=pltpu.SMEM)] * smem + [pl.BlockSpec(memory_space=pl.ANY)] * held
    shapes = [jax.ShapeDtypeStruct(shape, dtype) for shape, dtype in outs]
    moved = sum(math.prod(s.shape) * s.dtype.itemsize for s in [*shapes, *args[: near + smem]])

    def run(*refs):
        body(*refs[: near + smem], *refs[near + smem + held :])

    return pl.pallas_call(
        run,
        out_shape=shapes,
        in_specs=specs,
        out_specs=[pl.BlockSpec(memory_space=pltpu.VMEM)] * len(shapes),
        scratch_shapes=list(scratch),
        compiler_params=pltpu.CompilerParams(vmem_limit_bytes=vmem * 2**20),
        cost_estimate=pl.CostEstimate(flops=flops, bytes_accessed=0, transcendentals=0),
    )(*args)


def after(array, *awaited):
    return pl.pallas_call(
        lambda *refs: None,
        out_shape=jax.ShapeDtypeStruct(array.shape, array.dtype),
        in_specs=[pl.BlockSpec(memory_space=pl.ANY)] * (1 + len(awaited)),
        out_specs=pl.BlockSpec(memory_space=pl.ANY),
        input_output_aliases={0: 0},
        compiler_params=pltpu.CompilerParams(vmem_limit_bytes=2**20),
        cost_estimate=pl.CostEstimate(flops=0, bytes_accessed=0, transcendentals=0),
    )(array, *awaited)


def copy_all(sems, pairs):
    copies = [pltpu.make_async_copy(source, target, sems.at[n]) for n, (source, target) in enumerate(pairs)]
    for copy in copies:
        copy.start()
    for copy in copies:
        copy.wait()


BF16, F32 = jnp.bfloat16, jnp.float32


def local_pairs(query, keys, values, out_grad, normed_input, q_start, q_len):
    tokens = query.shape[1]
    width = HEADS * HEAD_DIM // 2
    kv_width = KV_HEADS * HEAD_DIM // 2
    own_heads = KV_HEADS // 2
    repeat_by = HEADS // KV_HEADS
    group_width = repeat_by * HEAD_DIM
    seq_len = 4 * tokens
    seen = seq_len * 7 // 8
    model = normed_input.shape[2]
    pair_rows = model // 4
    planes = lax.axis_size("dp")
    part_rows = pair_rows // 2 // planes
    score_scale = 1.0 / math.sqrt(HEAD_DIM)
    query, keys, values, out_grad, hidden = query[0], keys[0], values[0], out_grad[0], normed_input[0]

    def place():
        me = lax.axis_index("seq")
        return me % 2, me % 4, me // 4

    def split_pairs(key_ref, value_ref, kv_mine, kv_other, sems):
        core, _, _ = place()
        copy_all(
            sems,
            [
                (ref.at[:, lanes(half * kv_width, kv_width)], out.at[:, pl.ds(part * kv_width, kv_width)])
                for half, out in ((core, kv_mine), (1 - core, kv_other))
                for part, ref in enumerate((key_ref, value_ref))
            ],
        )

    kv_mine, kv_other = call(
        split_pairs,
        [((tokens, 2 * kv_width), BF16)] * 2,
        (keys, values),
        scratch=[pltpu.SemaphoreType.DMA((4,))],
        place=pl.ANY,
        vmem=60,
    )
    kv_far = swap(kv_mine, "seq", 2)
    kv_cross = swap(kv_other, "seq", 3)

    kv_pair = swap(kv_other, "seq", 1)
    query_pair = swap(query, "seq", 1)
    grad_pair = swap(out_grad, "seq", 1)

    def split_hidden(hidden_ref, *outs):
        *outs, sems = outs
        pair = lax.axis_index("seq") // 2
        copy_all(
            sems,
            [
                (hidden_ref.at[:, lanes(jnp.bitwise_xor(pair, flip) * pair_rows, pair_rows)], out)
                for flip, out in enumerate(outs)
            ],
        )

    hidden_send = call(
        split_hidden,
        [((tokens, pair_rows), BF16)] * 4,
        (hidden, kv_mine),
        scratch=[pltpu.SemaphoreType.DMA((4,))],
        held=1,
        place=pl.ANY,
    )
    hidden_core = {
        0: hidden_send[0],
        1: swap(after(hidden_send[1], query_pair), "seq", 2),
        2: swap(after(hidden_send[2], query_pair), "seq", 4),
        3: swap(after(hidden_send[3], query_pair), "seq", 6),
    }

    def attention(head, query_ref, grad_ref, query_far, grad_far, kv0, kv1, kv2, kv3, start_ref, len_ref, part, part_low, mine, other, key_all, value_all):
        core, spot, seq_idx = place()
        for flip, ref in enumerate((kv0, kv1, kv2, kv3)):
            rows = pl.ds(pl.multiple_of(jnp.bitwise_xor(spot, flip) * tokens, tokens), tokens)
            key_all[rows, :] = ref[:, head * HEAD_DIM : (head + 1) * HEAD_DIM]
            first = kv_width + head * HEAD_DIM
            value_all[rows, :] = ref[:, first : first + HEAD_DIM]
        key = key_all[:seen, :]
        value = value_all[:seen, :]
        start = start_ref[seq_idx]
        end = start + len_ref[seq_idx]
        columns = repeat_by * tokens
        row = lax.broadcasted_iota(jnp.int32, (1, columns), 1) % tokens
        key_pos = lax.broadcasted_iota(jnp.int32, (seen, columns), 0)
        for side, out in enumerate((mine, other)):
            blocks = [
                [ref[:, lanes(core * width + head * group_width + r * HEAD_DIM, HEAD_DIM)] for r in range(repeat_by)]
                for ref in ((query_ref, grad_ref), (query_far, grad_far))[side]
            ]
            query_rows = jnp.concatenate(blocks[0], axis=0)
            grad_rows = jnp.concatenate(blocks[1], axis=0)
            query_pos = jnp.bitwise_xor(spot, side) * tokens + row
            limit = jnp.minimum(end, jnp.maximum(start, query_pos + 1))
            scores = dot(key, query_rows, ((1,), (1,)))
            scores = jnp.where(key_pos < limit, scores, -jnp.inf)
            row_max = jnp.max(scores, axis=0, keepdims=True)
            exponent = jnp.exp((scores - row_max) * score_scale)
            probability = exponent * (1.0 / jnp.sum(exponent, axis=0, keepdims=True))
            dprob = dot(value, grad_rows, ((1,), (1,)))
            row_delta = jnp.sum(probability * dprob, axis=0, keepdims=True)
            dscore = (probability * (dprob - row_delta)).astype(BF16)
            key_part = dot(dscore, query_rows, ((1,), (0,))) * score_scale
            value_part = dot(probability.astype(BF16), grad_rows, ((1,), (0,)))
            if side == 0:
                part[:, :HEAD_DIM] = key_part
                part[:, HEAD_DIM:] = value_part
            else:
                part[:, :HEAD_DIM] += key_part
                part[:, HEAD_DIM:] += value_part
            query_grad = dot(key, dscore, ((0,), (0,))) * score_scale
            for r in range(repeat_by):
                out[:, r * HEAD_DIM : (r + 1) * HEAD_DIM] = query_grad[:, r * tokens : (r + 1) * tokens].T.astype(BF16)
        part_low[...] = part[...].astype(BF16)

    def add_parts(part, far, out):
        out[...] = (part[...] + far[...].astype(F32)).astype(BF16)

    def weight(*refs):
        *hidden_refs, own, other, kept, send = refs[:-2]
        rows = refs[-2:]
        _, spot, _ = place()
        plane = lax.axis_index("dp")
        padded, rows = rows[0], rows[1]
        padded[seen:, :] = jnp.zeros((seq_len - seen, 2 * HEAD_DIM), BF16)
        for flip in range(4):
            if flip % 2 == 0:
                padded[:seen, :] = (own, other)[flip // 2][...]
            for core in range(2):
                source = pl.multiple_of(jnp.bitwise_xor(spot, 2 * (flip % 2) + core) * tokens, tokens)
                target = (2 * flip + core) * tokens
                rows[target : target + tokens, :] = padded[pl.ds(source, tokens), :]
        grads = rows[...]
        for flip, out, half in ((1, send, 0), (3, send, 1), (0, kept, 0), (2, kept, 1)):
            target = jnp.bitwise_xor(plane, flip)
            for owner in range(2):
                spot = lanes((owner * planes + target) * part_rows, part_rows)
                hidden_part = jnp.concatenate([ref[:, spot] for ref in hidden_refs], axis=0)
                total = dot(hidden_part, grads, ((0,), (0,)))
                first = (2 * half + owner) * part_rows
                out[first : first + part_rows, :] = total.astype(out.dtype)

    def add_near(kept, near, out):
        out[...] = (kept[2 * part_rows :, :] + near[2 * part_rows :, :].astype(F32)).astype(BF16)

    grads, query_parts, weight_parts = [], [], []
    sums = []
    for head in range(own_heads):
        awaited = (hidden_core[1], hidden_core[2], query_parts[0][0]) if head else ()
        part, part_low, query_mine, query_other = call(
            functools.partial(attention, head),
            [
                ((seen, 2 * HEAD_DIM), F32),
                ((seen, 2 * HEAD_DIM), BF16),
                ((tokens, group_width), BF16),
                ((tokens, group_width), BF16),
            ],
            (query, out_grad, query_pair, grad_pair, kv_mine, kv_pair, kv_far, kv_cross, q_start, q_len, *awaited),
            scratch=[pltpu.VMEM((seq_len, HEAD_DIM), BF16)] * 2,
            smem=2,
            held=len(awaited),
            vmem=32,
            flops=10 * seen * 2 * group_width * tokens * (0 if head else 20),
        )
        query_parts.append((query_mine, query_other))
        if head:
            (grad,) = call(add_parts, [((seen, 2 * HEAD_DIM), BF16)], (*sums[0], query_mine, hidden_core[3]), held=2)
            sums[0] = (grad, swap(grad, "seq", 4))
        sums.append((part, swap(part_low, "seq", 2)))
    hidden_blocks = []
    for flip in range(4):
        block = hidden_core[flip]
        halves = (block[: tokens // 2], block[tokens // 2 :]) if flip == 3 else (block,)
        hidden_blocks += [block, *[swap(half, "seq", 1) for half in halves]]
    (grad,) = call(add_parts, [((seen, 2 * HEAD_DIM), BF16)], sums[1])
    sums[1] = (grad, swap(grad, "seq", 4))
    for head in range(own_heads):
        grads.append(sums[head][0])
        kept, send = call(
            weight,
            [((4 * part_rows, 2 * HEAD_DIM), F32), ((4 * part_rows, 2 * HEAD_DIM), BF16)],
            (*hidden_blocks, *sums[head]),
            scratch=[pltpu.VMEM((seq_len, 2 * HEAD_DIM), BF16), pltpu.VMEM((8 * tokens, 2 * HEAD_DIM), BF16)],
        )
        weight_parts.append((kept, swap(send, "dp", 1)))
    awaited = ()
    for head, (kept, near) in enumerate(weight_parts):
        (send,) = call(
            add_near,
            [((2 * part_rows, 2 * HEAD_DIM), BF16)],
            (kept, near, *awaited),
            held=len(awaited),
            flops=0 if head else 2000000000,
        )
        awaited = (send,)
        weight_parts[head] = (kept, near, swap(send, "dp", 2))

    def pack(grad0, grad1, other0, other1, send, kept):
        _, spot, _ = place()
        for head, (grad, other) in enumerate(((grad0, other0), (grad1, other1))):
            padded = jnp.concatenate([grad[...], jnp.zeros((seq_len - seen, 2 * HEAD_DIM), BF16)], axis=0)
            for ref, wanted in ((kept, spot), (send, jnp.bitwise_xor(spot, 1))):
                chosen = jnp.zeros((tokens, 2 * HEAD_DIM), BF16)
                for block in range(4):
                    chosen = jnp.where(wanted == block, padded[block * tokens : (block + 1) * tokens], chosen)
                ref[:, head * 2 * HEAD_DIM : (head + 1) * 2 * HEAD_DIM] = chosen
            send[:, 2 * kv_width + head * group_width : 2 * kv_width + (head + 1) * group_width] = other[...]

    send, kept = call(
        pack,
        [((tokens, 2 * kv_width + width), BF16), ((tokens, 2 * kv_width), BF16)],
        (*grads, query_parts[0][1], query_parts[1][1]),
    )
    got = swap(send, "seq", 1)

    def unpack(kept_ref, got_ref, mine0, mine1, query_out, key_out, value_out):
        core, _, _ = place()
        for head, mine in enumerate((mine0, mine1)):
            query_out[:, lanes(core * width + head * group_width, group_width)] = mine[...]
            first = 2 * kv_width + head * group_width
            query_out[:, lanes((1 - core) * width + head * group_width, group_width)] = got_ref[:, first : first + group_width]
            for ref, side in ((kept_ref, core), (got_ref, 1 - core)):
                spot = lanes(side * kv_width + head * HEAD_DIM, HEAD_DIM)
                first = head * 2 * HEAD_DIM
                key_out[:, spot] = ref[:, first : first + HEAD_DIM]
                value_out[:, spot] = ref[:, first + HEAD_DIM : first + 2 * HEAD_DIM]

    query_grad, key_grad, value_grad = call(
        unpack,
        [((tokens, 2 * width), BF16), ((tokens, 2 * kv_width), BF16), ((tokens, 2 * kv_width), BF16)],
        (kept, got, query_parts[0][0], query_parts[1][0]),
    )

    def add_planes(kept, near, far, kept_out, send_out):
        core, _, _ = place()
        for out, owner in ((kept_out, core), (send_out, 1 - core)):
            rows = pl.ds(pl.multiple_of(owner * part_rows, part_rows), part_rows)
            out[...] = kept[rows, :] + (near[rows, :].astype(F32) + far[rows, :].astype(F32))

    pieces = []
    for parts in weight_parts:
        kept_weight, send_weight = call(add_planes, [((part_rows, 2 * HEAD_DIM), F32)] * 2, parts)
        pieces += [kept_weight, swap(send_weight, "seq", 1)]

    def join(kept0, got0, kept1, got1, out):
        core, _, _ = place()
        for head, (kept_ref, got_ref) in enumerate(((kept0, got0), (kept1, got1))):
            for ref, side in ((kept_ref, core), (got_ref, 1 - core)):
                spot = side * kv_width + head * HEAD_DIM
                out[:, lanes(spot, HEAD_DIM)] = ref[:, :HEAD_DIM]
                out[:, lanes(2 * kv_width + spot, HEAD_DIM)] = ref[:, HEAD_DIM:]

    (weight_grad,) = call(join, [((part_rows, 4 * kv_width), F32)], pieces)
    return query_grad[None], key_grad[None], value_grad[None], weight_grad


def solution(mesh):
    in_specs = (
        P("dp", "seq", None),
        P("dp", "seq", None),
        P("dp", "seq", None),
        P("dp", "seq", None),
        P("dp", "seq", None),
        P("dp"),
        P("dp"),
    )
    out_specs = (
        P("dp", "seq", None),
        P("dp", "seq", None),
        P("dp", "seq", None),
        P(("seq", "dp"), None),
    )
    body = local_pairs if (mesh.shape["seq"], mesh.shape["dp"]) == (2 * KV_HEADS, 4) else local
    return jax.shard_map(body, mesh=mesh, in_specs=in_specs, out_specs=out_specs, check_vma=False)
```

```python
import functools
import math

import jax
import jax.numpy as jnp
from jax import lax
from jax.experimental import pallas as pl
from jax.experimental.pallas import tpu as pltpu
from jax.sharding import PartitionSpec as P

HEADS = 16
KV_HEADS = 4
HEAD_DIM = 128


def local(query, keys, values, out_grad, normed_input, q_start, q_len):
    seq_count = lax.axis_size("seq")
    tokens_dev = query.shape[1]
    repeat_by = HEADS // KV_HEADS
    classes = max(1, seq_count // HEADS)
    heads_dev = HEADS * classes // seq_count
    head_groups = seq_count // classes
    class_tokens = tokens_dev // classes
    seq_len = tokens_dev * seq_count // 2
    group_tokens = tokens_dev * seq_count
    width_dev = heads_dev * HEAD_DIM
    my_class = lax.axis_index("seq") // head_groups
    score_scale = 1.0 / math.sqrt(HEAD_DIM)

    def to_units(array):
        return array.reshape(class_tokens, seq_count, width_dev)

    query_units = to_units(query[0])
    grad_units = to_units(out_grad[0])
    key_wide = jnp.repeat(
        keys[0].reshape(tokens_dev, KV_HEADS, HEAD_DIM), repeat_by, axis=1
    ).reshape(tokens_dev, HEADS * HEAD_DIM)
    value_wide = jnp.repeat(
        values[0].reshape(tokens_dev, KV_HEADS, HEAD_DIM), repeat_by, axis=1
    ).reshape(tokens_dev, HEADS * HEAD_DIM)
    wide_shape = (tokens_dev, classes, head_groups, width_dev)
    key_units = jnp.broadcast_to(
        key_wide.reshape(tokens_dev, 1, head_groups, width_dev), wide_shape
    ).reshape(tokens_dev, seq_count, width_dev)
    value_units = jnp.broadcast_to(
        value_wide.reshape(tokens_dev, 1, head_groups, width_dev), wide_shape
    ).reshape(tokens_dev, seq_count, width_dev)
    query_got, grad_got, key_got, value_got = (
        lax.all_to_all(query_units, "seq", split_axis=1, concat_axis=0, tiled=True),
        lax.all_to_all(grad_units, "seq", split_axis=1, concat_axis=0, tiled=True),
        lax.all_to_all(key_units, "seq", split_axis=1, concat_axis=0, tiled=True),
        lax.all_to_all(value_units, "seq", split_axis=1, concat_axis=0, tiled=True),
    )
    key_rows = key_got.reshape(group_tokens, heads_dev, HEAD_DIM)
    value_rows = value_got.reshape(group_tokens, heads_dev, HEAD_DIM)
    query_rows = query_got.reshape(seq_count * class_tokens, heads_dev, HEAD_DIM)
    grad_rows = grad_got.reshape(seq_count * class_tokens, heads_dev, HEAD_DIM)
    block_rows = min(512, seq_len // classes)
    blocks_seq = seq_len // classes // block_rows
    key_pos = jnp.arange(seq_len, dtype=jnp.int32)

    def one_block(block_idx, carry):
        query_acc, key_acc, value_acc = carry
        seq_idx = block_idx // blocks_seq
        first_row = block_idx * block_rows
        key_first = seq_idx * seq_len
        query_block = lax.dynamic_slice_in_dim(query_rows, first_row, block_rows, 0)
        grad_block = lax.dynamic_slice_in_dim(grad_rows, first_row, block_rows, 0)
        key_block = lax.dynamic_slice_in_dim(key_rows, key_first, seq_len, 0)
        value_block = lax.dynamic_slice_in_dim(value_rows, key_first, seq_len, 0)
        start_pos = lax.dynamic_index_in_dim(q_start, seq_idx, 0, keepdims=False)
        end_pos = start_pos + lax.dynamic_index_in_dim(q_len, seq_idx, 0, keepdims=False)
        query_pos = (
            (first_row + jnp.arange(block_rows, dtype=jnp.int32)) * classes + my_class - key_first
        )
        visible = (key_pos[None, :] < end_pos) & (
            (key_pos[None, :] <= query_pos[:, None]) | (key_pos[None, :] < start_pos)
        )
        scores = (
            jnp.einsum("qhd,khd->hqk", query_block, key_block, preferred_element_type=jnp.float32)
            * score_scale
        )
        scores = jnp.where(visible[None], scores, -jnp.inf)
        row_max = jnp.max(scores, axis=-1, keepdims=True)
        exponent = jnp.where(visible[None], jnp.exp(scores - row_max), 0.0)
        probability = exponent / jnp.sum(exponent, axis=-1, keepdims=True)
        prob_low = probability.astype(jnp.bfloat16)
        dprob = jnp.einsum(
            "qhd,khd->hqk", grad_block, value_block, preferred_element_type=jnp.float32
        )
        row_delta = jnp.sum(probability * dprob, axis=-1, keepdims=True)
        dscore = (probability * (dprob - row_delta) * score_scale).astype(jnp.bfloat16)
        query_grad = jnp.einsum(
            "hqk,khd->qhd", dscore, key_block, preferred_element_type=jnp.float32
        ).astype(jnp.bfloat16)
        query_acc = lax.dynamic_update_slice_in_dim(query_acc, query_grad, first_row, 0)
        key_part = lax.dynamic_slice_in_dim(key_acc, key_first, seq_len, 0) + jnp.einsum(
            "hqk,qhd->khd", dscore, query_block, preferred_element_type=jnp.float32
        )
        value_part = lax.dynamic_slice_in_dim(value_acc, key_first, seq_len, 0) + jnp.einsum(
            "hqk,qhd->khd", prob_low, grad_block, preferred_element_type=jnp.float32
        )
        key_acc = lax.dynamic_update_slice_in_dim(key_acc, key_part, key_first, 0)
        value_acc = lax.dynamic_update_slice_in_dim(value_acc, value_part, key_first, 0)
        return (query_acc, key_acc, value_acc)

    start_state = (
        jnp.zeros((seq_count * class_tokens, heads_dev, HEAD_DIM), jnp.bfloat16),
        jnp.zeros((group_tokens, heads_dev, HEAD_DIM), jnp.float32),
        jnp.zeros((group_tokens, heads_dev, HEAD_DIM), jnp.float32),
    )
    query_acc, key_acc, value_acc = lax.fori_loop(0, 2 * blocks_seq, one_block, start_state)
    query_back = lax.all_to_all(
        query_acc.reshape(seq_count, class_tokens, 1, width_dev),
        "seq",
        split_axis=0,
        concat_axis=2,
        tiled=True,
    )
    query_grad_out = query_back.reshape(tokens_dev, HEADS * HEAD_DIM)
    key_back, value_back = (
        lax.all_to_all(
            key_acc.reshape(seq_count, tokens_dev, 1, width_dev).astype(jnp.bfloat16),
            "seq",
            split_axis=0,
            concat_axis=2,
            tiled=True,
        ).astype(jnp.float32),
        lax.all_to_all(
            value_acc.reshape(seq_count, tokens_dev, 1, width_dev).astype(jnp.bfloat16),
            "seq",
            split_axis=0,
            concat_axis=2,
            tiled=True,
        ).astype(jnp.float32),
    )
    key_grad_out = (
        key_back.reshape(tokens_dev, classes, KV_HEADS, repeat_by, HEAD_DIM)
        .sum(axis=(1, 3))
        .astype(jnp.bfloat16)
        .reshape(tokens_dev, KV_HEADS * HEAD_DIM)
    )
    value_grad_out = (
        value_back.reshape(tokens_dev, classes, KV_HEADS, repeat_by, HEAD_DIM)
        .sum(axis=(1, 3))
        .astype(jnp.bfloat16)
        .reshape(tokens_dev, KV_HEADS * HEAD_DIM)
    )
    joined = jnp.concatenate([key_grad_out, value_grad_out], axis=1)
    hidden_rows = normed_input[0]
    weight_out = lax.psum_scatter(
        jnp.einsum("tr,tc->rc", hidden_rows, joined, preferred_element_type=jnp.float32),
        ("seq", "dp"),
        scatter_dimension=0,
        tiled=True,
    )
    return (query_grad_out[None], key_grad_out[None], value_grad_out[None], weight_out)


def swap(array, axis, bit):
    size = lax.axis_size(axis)
    return lax.ppermute(array, axis, [(i, i ^ bit) for i in range(size)])


def dot(left, right, dims):
    return lax.dot_general(left, right, (dims, ((), ())), preferred_element_type=jnp.float32)


def lanes(start, width):
    return pl.ds(pl.multiple_of(start, 128), width)


def call(body, outs, args, scratch=(), smem=0, held=0, flops=0, vmem=16, place=pltpu.VMEM):
    near = len(args) - smem - held
    specs = [pl.BlockSpec(memory_space=place)] * near
    specs += [pl.BlockSpec(memory_space=pltpu.SMEM)] * smem + [pl.BlockSpec(memory_space=pl.ANY)] * held
    shapes = [jax.ShapeDtypeStruct(shape, dtype) for shape, dtype in outs]
    moved = sum(math.prod(s.shape) * s.dtype.itemsize for s in [*shapes, *args[: near + smem]])

    def run(*refs):
        body(*refs[: near + smem], *refs[near + smem + held :])

    return pl.pallas_call(
        run,
        out_shape=shapes,
        in_specs=specs,
        out_specs=[pl.BlockSpec(memory_space=pltpu.VMEM)] * len(shapes),
        scratch_shapes=list(scratch),
        compiler_params=pltpu.CompilerParams(vmem_limit_bytes=vmem * 2**20),
        cost_estimate=pl.CostEstimate(flops=flops, bytes_accessed=0, transcendentals=0),
    )(*args)


def after(array, *awaited):
    return pl.pallas_call(
        lambda *refs: None,
        out_shape=jax.ShapeDtypeStruct(array.shape, array.dtype),
        in_specs=[pl.BlockSpec(memory_space=pl.ANY)] * (1 + len(awaited)),
        out_specs=pl.BlockSpec(memory_space=pl.ANY),
        input_output_aliases={0: 0},
        compiler_params=pltpu.CompilerParams(vmem_limit_bytes=2**20),
        cost_estimate=pl.CostEstimate(flops=0, bytes_accessed=0, transcendentals=0),
    )(array, *awaited)


def copy_all(sems, pairs):
    copies = [pltpu.make_async_copy(source, target, sems.at[n]) for n, (source, target) in enumerate(pairs)]
    for copy in copies:
        copy.start()
    for copy in copies:
        copy.wait()


BF16, F32 = jnp.bfloat16, jnp.float32


def local_pairs(query, keys, values, out_grad, normed_input, q_start, q_len):
    tokens = query.shape[1]
    width = HEADS * HEAD_DIM // 2
    kv_width = KV_HEADS * HEAD_DIM // 2
    own_heads = KV_HEADS // 2
    repeat_by = HEADS // KV_HEADS
    group_width = repeat_by * HEAD_DIM
    seq_len = 4 * tokens
    seen = seq_len * 7 // 8
    model = normed_input.shape[2]
    pair_rows = model // 4
    planes = lax.axis_size("dp")
    part_rows = pair_rows // 2 // planes
    score_scale = 1.0 / math.sqrt(HEAD_DIM)
    query, keys, values, out_grad, hidden = query[0], keys[0], values[0], out_grad[0], normed_input[0]

    def place():
        me = lax.axis_index("seq")
        return me % 2, me % 4, me // 4

    pairs = {0: (keys, values), 2: (swap(keys, "seq", 2), swap(values, "seq", 2))}
    query_pair, grad_pair = swap(query, "seq", 1), swap(out_grad, "seq", 1)
    for flip in (0, 2):
        pairs[flip + 1] = tuple(swap(array, "seq", 1) for array in pairs[flip])
    key_blocks, value_blocks = zip(*(pairs[flip] for flip in range(4)))

    def split_hidden(hidden_ref, *outs):
        *outs, sems = outs
        pair = lax.axis_index("seq") // 2
        copy_all(
            sems,
            [
                (hidden_ref.at[:, lanes(jnp.bitwise_xor(pair, flip) * pair_rows, pair_rows)], out)
                for flip, out in enumerate(outs)
            ],
        )

    hidden_send = call(
        split_hidden,
        [((tokens, pair_rows), BF16)] * 4,
        (hidden,),
        scratch=[pltpu.SemaphoreType.DMA((4,))],
        place=pl.ANY,
    )
    hidden_core = {
        0: hidden_send[0],
        1: swap(after(hidden_send[1], query_pair), "seq", 2),
        2: swap(after(hidden_send[2], query_pair), "seq", 4),
        3: swap(after(hidden_send[3], query_pair), "seq", 6),
    }

    hidden_pair = {flip: swap(hidden_core[flip], "seq", 1) for flip in (0, 1, 2)}

    def attention(head, *refs):
        query_ref, grad_ref, query_far, grad_far, *pair_refs = refs[:12]
        start_ref, len_ref, part, part_low, mine, other, key_all, value_all = refs[12:]
        core, spot, seq_idx = place()
        for flip in range(4):
            rows = pl.ds(pl.multiple_of(jnp.bitwise_xor(spot, flip) * tokens, tokens), tokens)
            columns = lanes(core * kv_width + head * HEAD_DIM, HEAD_DIM)
            key_all[rows, :] = pair_refs[flip][:, columns]
            value_all[rows, :] = pair_refs[4 + flip][:, columns]
        key = key_all[:seen, :]
        value = value_all[:seen, :]
        start = start_ref[seq_idx]
        end = start + len_ref[seq_idx]
        columns = repeat_by * tokens
        row = lax.broadcasted_iota(jnp.int32, (1, columns), 1) % tokens
        key_pos = lax.broadcasted_iota(jnp.int32, (seen, columns), 0)
        for side, out in enumerate((mine, other)):
            blocks = [
                [ref[:, lanes(core * width + head * group_width + r * HEAD_DIM, HEAD_DIM)] for r in range(repeat_by)]
                for ref in ((query_ref, grad_ref), (query_far, grad_far))[side]
            ]
            query_rows = jnp.concatenate(blocks[0], axis=0)
            grad_rows = jnp.concatenate(blocks[1], axis=0)
            query_pos = jnp.bitwise_xor(spot, side) * tokens + row
            limit = jnp.minimum(end, jnp.maximum(start, query_pos + 1))
            scores = dot(key, query_rows, ((1,), (1,)))
            scores = jnp.where(key_pos < limit, scores, -jnp.inf)
            row_max = jnp.max(scores, axis=0, keepdims=True)
            exponent = jnp.exp((scores - row_max) * score_scale)
            probability = exponent * (1.0 / jnp.sum(exponent, axis=0, keepdims=True))
            dprob = dot(value, grad_rows, ((1,), (1,)))
            row_delta = jnp.sum(probability * dprob, axis=0, keepdims=True)
            dscore = (probability * (dprob - row_delta)).astype(BF16)
            key_part = dot(dscore, query_rows, ((1,), (0,))) * score_scale
            value_part = dot(probability.astype(BF16), grad_rows, ((1,), (0,)))
            if side == 0:
                part[:, :HEAD_DIM] = key_part
                part[:, HEAD_DIM:] = value_part
            else:
                part[:, :HEAD_DIM] += key_part
                part[:, HEAD_DIM:] += value_part
            query_grad = dot(key, dscore, ((0,), (0,))) * score_scale
            for r in range(repeat_by):
                out[:, r * HEAD_DIM : (r + 1) * HEAD_DIM] = query_grad[:, r * tokens : (r + 1) * tokens].T.astype(BF16)
        part_low[...] = part[...].astype(BF16)

    def add_parts(part, far, out):
        out[...] = (part[...] + far[...].astype(F32)).astype(BF16)

    def weight(*refs):
        *hidden_refs, own, other, kept, send = refs[:-2]
        rows = refs[-2:]
        _, spot, _ = place()
        plane = lax.axis_index("dp")
        padded, rows = rows[0], rows[1]
        padded[seen:, :] = jnp.zeros((seq_len - seen, 2 * HEAD_DIM), BF16)
        for flip in range(4):
            if flip % 2 == 0:
                padded[:seen, :] = (own, other)[flip // 2][...]
            for core in range(2):
                source = pl.multiple_of(jnp.bitwise_xor(spot, 2 * (flip % 2) + core) * tokens, tokens)
                target = (2 * flip + core) * tokens
                rows[target : target + tokens, :] = padded[pl.ds(source, tokens), :]
        grads = rows[...]
        for flip, out, half in ((1, send, 0), (3, send, 1), (0, kept, 0), (2, kept, 1)):
            target = jnp.bitwise_xor(plane, flip)
            for owner in range(2):
                spot = lanes((owner * planes + target) * part_rows, part_rows)
                hidden_part = jnp.concatenate([ref[:, spot] for ref in hidden_refs], axis=0)
                total = dot(hidden_part, grads, ((0,), (0,)))
                first = (2 * half + owner) * part_rows
                out[first : first + part_rows, :] = total.astype(out.dtype)

    def add_near(kept, near, out):
        out[...] = (kept[2 * part_rows :, :] + near[2 * part_rows :, :].astype(F32)).astype(BF16)

    grads, query_parts, weight_parts = [], [], []
    sums = []
    for head in range(own_heads):
        awaited = (hidden_pair[1], hidden_pair[2], query_parts[0][0]) if head else ()
        part, part_low, query_mine, query_other = call(
            functools.partial(attention, head),
            [
                ((seen, 2 * HEAD_DIM), F32),
                ((seen, 2 * HEAD_DIM), BF16),
                ((tokens, group_width), BF16),
                ((tokens, group_width), BF16),
            ],
            (query, out_grad, query_pair, grad_pair, *key_blocks, *value_blocks, q_start, q_len, *awaited),
            scratch=[pltpu.VMEM((seq_len, HEAD_DIM), BF16)] * 2,
            smem=2,
            held=len(awaited),
            vmem=32,
            flops=10 * seen * 2 * group_width * tokens * (0 if head else 2),
        )
        query_parts.append((query_mine, query_other))
        if head:
            (grad,) = call(add_parts, [((seen, 2 * HEAD_DIM), BF16)], (*sums[0], query_mine, hidden_core[3]), held=2)
            sums[0] = (grad, swap(grad, "seq", 4))
        sums.append((part, swap(part_low, "seq", 2)))
    halves = [swap(half, "seq", 1) for half in (hidden_core[3][: tokens // 2], hidden_core[3][tokens // 2 :])]
    hidden_blocks = [block for flip in (0, 1, 2) for block in (hidden_core[flip], hidden_pair[flip])]
    hidden_blocks += [hidden_core[3], *halves]
    (grad,) = call(add_parts, [((seen, 2 * HEAD_DIM), BF16)], sums[1])
    sums[1] = (grad, swap(grad, "seq", 4))
    for head in range(own_heads):
        grads.append(sums[head][0])
        kept, send = call(
            weight,
            [((4 * part_rows, 2 * HEAD_DIM), F32), ((4 * part_rows, 2 * HEAD_DIM), BF16)],
            (*hidden_blocks, *sums[head]),
            scratch=[pltpu.VMEM((seq_len, 2 * HEAD_DIM), BF16), pltpu.VMEM((8 * tokens, 2 * HEAD_DIM), BF16)],
        )
        weight_parts.append((kept, swap(send, "dp", 1)))
    awaited = ()
    for head, (kept, near) in enumerate(weight_parts):
        (send,) = call(
            add_near,
            [((2 * part_rows, 2 * HEAD_DIM), BF16)],
            (kept, near, *awaited),
            held=len(awaited),
            flops=0 if head else 2000000000,
        )
        awaited = (send,)
        weight_parts[head] = (kept, near, swap(send, "dp", 2))

    def pack(grad0, grad1, other0, other1, send, kept):
        _, spot, _ = place()
        for head, (grad, other) in enumerate(((grad0, other0), (grad1, other1))):
            padded = jnp.concatenate([grad[...], jnp.zeros((seq_len - seen, 2 * HEAD_DIM), BF16)], axis=0)
            for ref, wanted in ((kept, spot), (send, jnp.bitwise_xor(spot, 1))):
                chosen = jnp.zeros((tokens, 2 * HEAD_DIM), BF16)
                for block in range(4):
                    chosen = jnp.where(wanted == block, padded[block * tokens : (block + 1) * tokens], chosen)
                ref[:, head * 2 * HEAD_DIM : (head + 1) * 2 * HEAD_DIM] = chosen
            send[:, 2 * kv_width + head * group_width : 2 * kv_width + (head + 1) * group_width] = other[...]

    send, kept = call(
        pack,
        [((tokens, 2 * kv_width + width), BF16), ((tokens, 2 * kv_width), BF16)],
        (*grads, query_parts[0][1], query_parts[1][1]),
    )
    got = swap(send, "seq", 1)

    def unpack(kept_ref, got_ref, mine0, mine1, query_out, key_out, value_out):
        core, _, _ = place()
        for head, mine in enumerate((mine0, mine1)):
            query_out[:, lanes(core * width + head * group_width, group_width)] = mine[...]
            first = 2 * kv_width + head * group_width
            query_out[:, lanes((1 - core) * width + head * group_width, group_width)] = got_ref[:, first : first + group_width]
            for ref, side in ((kept_ref, core), (got_ref, 1 - core)):
                spot = lanes(side * kv_width + head * HEAD_DIM, HEAD_DIM)
                first = head * 2 * HEAD_DIM
                key_out[:, spot] = ref[:, first : first + HEAD_DIM]
                value_out[:, spot] = ref[:, first + HEAD_DIM : first + 2 * HEAD_DIM]

    query_grad, key_grad, value_grad = call(
        unpack,
        [((tokens, 2 * width), BF16), ((tokens, 2 * kv_width), BF16), ((tokens, 2 * kv_width), BF16)],
        (kept, got, query_parts[0][0], query_parts[1][0]),
    )

    def add_planes(kept, near, far, kept_out, send_out):
        core, _, _ = place()
        for out, owner in ((kept_out, core), (send_out, 1 - core)):
            rows = pl.ds(pl.multiple_of(owner * part_rows, part_rows), part_rows)
            out[...] = kept[rows, :] + (near[rows, :].astype(F32) + far[rows, :].astype(F32))

    pieces = []
    for parts in weight_parts:
        kept_weight, send_weight = call(add_planes, [((part_rows, 2 * HEAD_DIM), F32)] * 2, parts)
        pieces += [kept_weight, swap(send_weight, "seq", 1)]

    def join(kept0, got0, kept1, got1, out):
        core, _, _ = place()
        for head, (kept_ref, got_ref) in enumerate(((kept0, got0), (kept1, got1))):
            for ref, side in ((kept_ref, core), (got_ref, 1 - core)):
                spot = side * kv_width + head * HEAD_DIM
                out[:, lanes(spot, HEAD_DIM)] = ref[:, :HEAD_DIM]
                out[:, lanes(2 * kv_width + spot, HEAD_DIM)] = ref[:, HEAD_DIM:]

    (weight_grad,) = call(join, [((part_rows, 4 * kv_width), F32)], pieces)
    return query_grad[None], key_grad[None], value_grad[None], weight_grad


def solution(mesh):
    in_specs = (
        P("dp", "seq", None),
        P("dp", "seq", None),
        P("dp", "seq", None),
        P("dp", "seq", None),
        P("dp", "seq", None),
        P("dp"),
        P("dp"),
    )
    out_specs = (
        P("dp", "seq", None),
        P("dp", "seq", None),
        P("dp", "seq", None),
        P(("seq", "dp"), None),
    )
    body = local_pairs if (mesh.shape["seq"], mesh.shape["dp"]) == (2 * KV_HEADS, 4) else local
    return jax.shard_map(body, mesh=mesh, in_specs=in_specs, out_specs=out_specs, check_vma=False)
```

```python
import functools
import math

import jax
import jax.numpy as jnp
from jax import lax
from jax.experimental import pallas as pl
from jax.experimental.pallas import tpu as pltpu
from jax.sharding import PartitionSpec as P

HEADS = 16
KV_HEADS = 4
HEAD_DIM = 128


def local(query, keys, values, out_grad, normed_input, q_start, q_len):
    seq_count = lax.axis_size("seq")
    tokens_dev = query.shape[1]
    repeat_by = HEADS // KV_HEADS
    classes = max(1, seq_count // HEADS)
    heads_dev = HEADS * classes // seq_count
    head_groups = seq_count // classes
    class_tokens = tokens_dev // classes
    seq_len = tokens_dev * seq_count // 2
    group_tokens = tokens_dev * seq_count
    width_dev = heads_dev * HEAD_DIM
    my_class = lax.axis_index("seq") // head_groups
    score_scale = 1.0 / math.sqrt(HEAD_DIM)

    def to_units(array):
        return array.reshape(class_tokens, seq_count, width_dev)

    query_units = to_units(query[0])
    grad_units = to_units(out_grad[0])
    key_wide = jnp.repeat(
        keys[0].reshape(tokens_dev, KV_HEADS, HEAD_DIM), repeat_by, axis=1
    ).reshape(tokens_dev, HEADS * HEAD_DIM)
    value_wide = jnp.repeat(
        values[0].reshape(tokens_dev, KV_HEADS, HEAD_DIM), repeat_by, axis=1
    ).reshape(tokens_dev, HEADS * HEAD_DIM)
    wide_shape = (tokens_dev, classes, head_groups, width_dev)
    key_units = jnp.broadcast_to(
        key_wide.reshape(tokens_dev, 1, head_groups, width_dev), wide_shape
    ).reshape(tokens_dev, seq_count, width_dev)
    value_units = jnp.broadcast_to(
        value_wide.reshape(tokens_dev, 1, head_groups, width_dev), wide_shape
    ).reshape(tokens_dev, seq_count, width_dev)
    query_got, grad_got, key_got, value_got = (
        lax.all_to_all(query_units, "seq", split_axis=1, concat_axis=0, tiled=True),
        lax.all_to_all(grad_units, "seq", split_axis=1, concat_axis=0, tiled=True),
        lax.all_to_all(key_units, "seq", split_axis=1, concat_axis=0, tiled=True),
        lax.all_to_all(value_units, "seq", split_axis=1, concat_axis=0, tiled=True),
    )
    key_rows = key_got.reshape(group_tokens, heads_dev, HEAD_DIM)
    value_rows = value_got.reshape(group_tokens, heads_dev, HEAD_DIM)
    query_rows = query_got.reshape(seq_count * class_tokens, heads_dev, HEAD_DIM)
    grad_rows = grad_got.reshape(seq_count * class_tokens, heads_dev, HEAD_DIM)
    block_rows = min(512, seq_len // classes)
    blocks_seq = seq_len // classes // block_rows
    key_pos = jnp.arange(seq_len, dtype=jnp.int32)

    def one_block(block_idx, carry):
        query_acc, key_acc, value_acc = carry
        seq_idx = block_idx // blocks_seq
        first_row = block_idx * block_rows
        key_first = seq_idx * seq_len
        query_block = lax.dynamic_slice_in_dim(query_rows, first_row, block_rows, 0)
        grad_block = lax.dynamic_slice_in_dim(grad_rows, first_row, block_rows, 0)
        key_block = lax.dynamic_slice_in_dim(key_rows, key_first, seq_len, 0)
        value_block = lax.dynamic_slice_in_dim(value_rows, key_first, seq_len, 0)
        start_pos = lax.dynamic_index_in_dim(q_start, seq_idx, 0, keepdims=False)
        end_pos = start_pos + lax.dynamic_index_in_dim(q_len, seq_idx, 0, keepdims=False)
        query_pos = (
            (first_row + jnp.arange(block_rows, dtype=jnp.int32)) * classes + my_class - key_first
        )
        visible = (key_pos[None, :] < end_pos) & (
            (key_pos[None, :] <= query_pos[:, None]) | (key_pos[None, :] < start_pos)
        )
        scores = (
            jnp.einsum("qhd,khd->hqk", query_block, key_block, preferred_element_type=jnp.float32)
            * score_scale
        )
        scores = jnp.where(visible[None], scores, -jnp.inf)
        row_max = jnp.max(scores, axis=-1, keepdims=True)
        exponent = jnp.where(visible[None], jnp.exp(scores - row_max), 0.0)
        probability = exponent / jnp.sum(exponent, axis=-1, keepdims=True)
        prob_low = probability.astype(jnp.bfloat16)
        dprob = jnp.einsum(
            "qhd,khd->hqk", grad_block, value_block, preferred_element_type=jnp.float32
        )
        row_delta = jnp.sum(probability * dprob, axis=-1, keepdims=True)
        dscore = (probability * (dprob - row_delta) * score_scale).astype(jnp.bfloat16)
        query_grad = jnp.einsum(
            "hqk,khd->qhd", dscore, key_block, preferred_element_type=jnp.float32
        ).astype(jnp.bfloat16)
        query_acc = lax.dynamic_update_slice_in_dim(query_acc, query_grad, first_row, 0)
        key_part = lax.dynamic_slice_in_dim(key_acc, key_first, seq_len, 0) + jnp.einsum(
            "hqk,qhd->khd", dscore, query_block, preferred_element_type=jnp.float32
        )
        value_part = lax.dynamic_slice_in_dim(value_acc, key_first, seq_len, 0) + jnp.einsum(
            "hqk,qhd->khd", prob_low, grad_block, preferred_element_type=jnp.float32
        )
        key_acc = lax.dynamic_update_slice_in_dim(key_acc, key_part, key_first, 0)
        value_acc = lax.dynamic_update_slice_in_dim(value_acc, value_part, key_first, 0)
        return (query_acc, key_acc, value_acc)

    start_state = (
        jnp.zeros((seq_count * class_tokens, heads_dev, HEAD_DIM), jnp.bfloat16),
        jnp.zeros((group_tokens, heads_dev, HEAD_DIM), jnp.float32),
        jnp.zeros((group_tokens, heads_dev, HEAD_DIM), jnp.float32),
    )
    query_acc, key_acc, value_acc = lax.fori_loop(0, 2 * blocks_seq, one_block, start_state)
    query_back = lax.all_to_all(
        query_acc.reshape(seq_count, class_tokens, 1, width_dev),
        "seq",
        split_axis=0,
        concat_axis=2,
        tiled=True,
    )
    query_grad_out = query_back.reshape(tokens_dev, HEADS * HEAD_DIM)
    key_back, value_back = (
        lax.all_to_all(
            key_acc.reshape(seq_count, tokens_dev, 1, width_dev).astype(jnp.bfloat16),
            "seq",
            split_axis=0,
            concat_axis=2,
            tiled=True,
        ).astype(jnp.float32),
        lax.all_to_all(
            value_acc.reshape(seq_count, tokens_dev, 1, width_dev).astype(jnp.bfloat16),
            "seq",
            split_axis=0,
            concat_axis=2,
            tiled=True,
        ).astype(jnp.float32),
    )
    key_grad_out = (
        key_back.reshape(tokens_dev, classes, KV_HEADS, repeat_by, HEAD_DIM)
        .sum(axis=(1, 3))
        .astype(jnp.bfloat16)
        .reshape(tokens_dev, KV_HEADS * HEAD_DIM)
    )
    value_grad_out = (
        value_back.reshape(tokens_dev, classes, KV_HEADS, repeat_by, HEAD_DIM)
        .sum(axis=(1, 3))
        .astype(jnp.bfloat16)
        .reshape(tokens_dev, KV_HEADS * HEAD_DIM)
    )
    joined = jnp.concatenate([key_grad_out, value_grad_out], axis=1)
    hidden_rows = normed_input[0]
    weight_out = lax.psum_scatter(
        jnp.einsum("tr,tc->rc", hidden_rows, joined, preferred_element_type=jnp.float32),
        ("seq", "dp"),
        scatter_dimension=0,
        tiled=True,
    )
    return (query_grad_out[None], key_grad_out[None], value_grad_out[None], weight_out)


def swap(array, axis, bit):
    size = lax.axis_size(axis)
    return lax.ppermute(array, axis, [(i, i ^ bit) for i in range(size)])


def dot(left, right, dims):
    return lax.dot_general(left, right, (dims, ((), ())), preferred_element_type=jnp.float32)


def lanes(start, width):
    return pl.ds(pl.multiple_of(start, 128), width)


def call(body, outs, args, scratch=(), smem=0, held=0, flops=0, vmem=16, place=pltpu.VMEM):
    near = len(args) - smem - held
    specs = [pl.BlockSpec(memory_space=place)] * near
    specs += [pl.BlockSpec(memory_space=pltpu.SMEM)] * smem + [pl.BlockSpec(memory_space=pl.ANY)] * held
    shapes = [jax.ShapeDtypeStruct(shape, dtype) for shape, dtype in outs]
    moved = sum(math.prod(s.shape) * s.dtype.itemsize for s in [*shapes, *args[: near + smem]])

    def run(*refs):
        body(*refs[: near + smem], *refs[near + smem + held :])

    return pl.pallas_call(
        run,
        out_shape=shapes,
        in_specs=specs,
        out_specs=[pl.BlockSpec(memory_space=pltpu.VMEM)] * len(shapes),
        scratch_shapes=list(scratch),
        compiler_params=pltpu.CompilerParams(vmem_limit_bytes=vmem * 2**20),
        cost_estimate=pl.CostEstimate(flops=flops, bytes_accessed=0, transcendentals=0),
    )(*args)


def after(array, *awaited):
    return pl.pallas_call(
        lambda *refs: None,
        out_shape=jax.ShapeDtypeStruct(array.shape, array.dtype),
        in_specs=[pl.BlockSpec(memory_space=pl.ANY)] * (1 + len(awaited)),
        out_specs=pl.BlockSpec(memory_space=pl.ANY),
        input_output_aliases={0: 0},
        compiler_params=pltpu.CompilerParams(vmem_limit_bytes=2**20),
        cost_estimate=pl.CostEstimate(flops=0, bytes_accessed=0, transcendentals=0),
    )(array, *awaited)


def copy_all(sems, pairs):
    copies = [pltpu.make_async_copy(source, target, sems.at[n]) for n, (source, target) in enumerate(pairs)]
    for copy in copies:
        copy.start()
    for copy in copies:
        copy.wait()


BF16, F32 = jnp.bfloat16, jnp.float32


def local_pairs(query, keys, values, out_grad, normed_input, q_start, q_len):
    tokens = query.shape[1]
    width = HEADS * HEAD_DIM // 2
    kv_width = KV_HEADS * HEAD_DIM // 2
    own_heads = KV_HEADS // 2
    repeat_by = HEADS // KV_HEADS
    group_width = repeat_by * HEAD_DIM
    seq_len = 4 * tokens
    seen = seq_len * 7 // 8
    model = normed_input.shape[2]
    pair_rows = model // 4
    planes = lax.axis_size("dp")
    part_rows = pair_rows // 2 // planes
    score_scale = 1.0 / math.sqrt(HEAD_DIM)
    query, keys, values, out_grad, hidden = query[0], keys[0], values[0], out_grad[0], normed_input[0]

    def place():
        me = lax.axis_index("seq")
        return me % 2, me % 4, me // 4

    pairs = {0: (keys, values), 2: (swap(keys, "seq", 2), swap(values, "seq", 2))}
    query_pair, grad_pair = swap(query, "seq", 1), swap(out_grad, "seq", 1)
    for flip in (0, 2):
        pairs[flip + 1] = tuple(swap(array, "seq", 1) for array in pairs[flip])
    key_blocks, value_blocks = zip(*(pairs[flip] for flip in range(4)))

    def split_hidden(hidden_ref, *outs):
        *outs, sems = outs
        pair = lax.axis_index("seq") // 2
        copy_all(
            sems,
            [
                (hidden_ref.at[:, lanes(jnp.bitwise_xor(pair, flip) * pair_rows, pair_rows)], out)
                for flip, out in enumerate(outs)
            ],
        )

    hidden_send = call(
        split_hidden,
        [((tokens, pair_rows), BF16)] * 4,
        (hidden,),
        scratch=[pltpu.SemaphoreType.DMA((4,))],
        place=pl.ANY,
    )
    hidden_core = {
        0: hidden_send[0],
        1: swap(after(hidden_send[1], query_pair), "seq", 2),
        2: swap(after(hidden_send[2], query_pair), "seq", 4),
        3: swap(after(hidden_send[3], query_pair), "seq", 6),
    }

    hidden_pair = {flip: swap(hidden_core[flip], "seq", 1) for flip in (0, 1, 2)}

    def attention(head, *refs):
        query_ref, grad_ref, query_far, grad_far, *pair_refs = refs[:12]
        start_ref, len_ref, part, part_low, mine, other, key_all, value_all = refs[12:]
        core, spot, seq_idx = place()
        for flip in range(4):
            rows = pl.ds(pl.multiple_of(jnp.bitwise_xor(spot, flip) * tokens, tokens), tokens)
            columns = lanes(core * kv_width + head * HEAD_DIM, HEAD_DIM)
            key_all[rows, :] = pair_refs[flip][:, columns]
            value_all[rows, :] = pair_refs[4 + flip][:, columns]
        key = key_all[:seen, :]
        value = value_all[:seen, :]
        start = start_ref[seq_idx]
        end = start + len_ref[seq_idx]
        columns = repeat_by * tokens
        row = lax.broadcasted_iota(jnp.int32, (1, columns), 1) % tokens
        key_pos = lax.broadcasted_iota(jnp.int32, (seen, columns), 0)
        for side, out in enumerate((mine, other)):
            blocks = [
                [ref[:, lanes(core * width + head * group_width + r * HEAD_DIM, HEAD_DIM)] for r in range(repeat_by)]
                for ref in ((query_ref, grad_ref), (query_far, grad_far))[side]
            ]
            query_rows = jnp.concatenate(blocks[0], axis=0)
            grad_rows = jnp.concatenate(blocks[1], axis=0)
            query_pos = jnp.bitwise_xor(spot, side) * tokens + row
            limit = jnp.minimum(end, jnp.maximum(start, query_pos + 1))
            scores = dot(key, query_rows, ((1,), (1,)))
            scores = jnp.where(key_pos < limit, scores, -jnp.inf)
            row_max = jnp.max(scores, axis=0, keepdims=True)
            exponent = jnp.exp2((scores - row_max) * (score_scale * math.log2(math.e)))
            probability = exponent * (1.0 / jnp.sum(exponent, axis=0, keepdims=True))
            dprob = dot(value, grad_rows, ((1,), (1,)))
            row_delta = jnp.sum(probability * dprob, axis=0, keepdims=True)
            dscore = (probability * (dprob - row_delta)).astype(BF16)
            key_part = dot(dscore, query_rows, ((1,), (0,))) * score_scale
            value_part = dot(probability.astype(BF16), grad_rows, ((1,), (0,)))
            if side == 0:
                part[:, :HEAD_DIM] = key_part
                part[:, HEAD_DIM:] = value_part
            else:
                part[:, :HEAD_DIM] += key_part
                part[:, HEAD_DIM:] += value_part
            query_grad = dot(key, dscore, ((0,), (0,))) * score_scale
            for r in range(repeat_by):
                out[:, r * HEAD_DIM : (r + 1) * HEAD_DIM] = query_grad[:, r * tokens : (r + 1) * tokens].T.astype(BF16)
        part_low[...] = part[...].astype(BF16)

    def add_parts(part, far, out):
        out[...] = (part[...] + far[...].astype(F32)).astype(BF16)

    def weight(*refs):
        *hidden_refs, own, other, kept, send = refs[:-2]
        rows = refs[-2:]
        _, spot, _ = place()
        plane = lax.axis_index("dp")
        padded, rows = rows[0], rows[1]
        padded[seen:, :] = jnp.zeros((seq_len - seen, 2 * HEAD_DIM), BF16)
        for flip in range(4):
            if flip % 2 == 0:
                padded[:seen, :] = (own, other)[flip // 2][...]
            for core in range(2):
                source = pl.multiple_of(jnp.bitwise_xor(spot, 2 * (flip % 2) + core) * tokens, tokens)
                target = (2 * flip + core) * tokens
                rows[target : target + tokens, :] = padded[pl.ds(source, tokens), :]
        grads = rows[...]
        for flip, out, half in ((1, send, 0), (3, send, 1), (0, kept, 0), (2, kept, 1)):
            target = jnp.bitwise_xor(plane, flip)
            for owner in range(2):
                spot = lanes((owner * planes + target) * part_rows, part_rows)
                hidden_part = jnp.concatenate([ref[:, spot] for ref in hidden_refs], axis=0)
                total = dot(hidden_part, grads, ((0,), (0,)))
                first = (2 * half + owner) * part_rows
                out[first : first + part_rows, :] = total.astype(out.dtype)

    def add_near(kept, near, out):
        out[...] = (kept[2 * part_rows :, :] + near[2 * part_rows :, :].astype(F32)).astype(BF16)

    grads, query_parts, weight_parts = [], [], []
    sums = []
    for head in range(own_heads):
        awaited = (hidden_pair[1], hidden_pair[2], query_parts[0][0]) if head else ()
        part, part_low, query_mine, query_other = call(
            functools.partial(attention, head),
            [
                ((seen, 2 * HEAD_DIM), F32),
                ((seen, 2 * HEAD_DIM), BF16),
                ((tokens, group_width), BF16),
                ((tokens, group_width), BF16),
            ],
            (query, out_grad, query_pair, grad_pair, *key_blocks, *value_blocks, q_start, q_len, *awaited),
            scratch=[pltpu.VMEM((seq_len, HEAD_DIM), BF16)] * 2,
            smem=2,
            held=len(awaited),
            vmem=32,
            flops=10 * seen * 2 * group_width * tokens * (0 if head else 2),
        )
        query_parts.append((query_mine, query_other))
        if head:
            (grad,) = call(add_parts, [((seen, 2 * HEAD_DIM), BF16)], (*sums[0], query_mine), held=1, flops=0)
            sums[0] = (grad, swap(grad, "seq", 4))
        sums.append((part, swap(part_low, "seq", 2)))
    halves = [swap(half, "seq", 1) for half in (hidden_core[3][: tokens // 2], hidden_core[3][tokens // 2 :])]
    hidden_blocks = [block for flip in (0, 1, 2) for block in (hidden_core[flip], hidden_pair[flip])]
    hidden_blocks += [hidden_core[3], *halves]
    (grad,) = call(add_parts, [((seen, 2 * HEAD_DIM), BF16)], sums[1])
    sums[1] = (grad, swap(grad, "seq", 4))
    for head in range(own_heads):
        grads.append(sums[head][0])
        kept, send = call(
            weight,
            [((4 * part_rows, 2 * HEAD_DIM), F32), ((4 * part_rows, 2 * HEAD_DIM), BF16)],
            (*hidden_blocks, *sums[head]),
            scratch=[pltpu.VMEM((seq_len, 2 * HEAD_DIM), BF16), pltpu.VMEM((8 * tokens, 2 * HEAD_DIM), BF16)],
        )
        weight_parts.append((kept, swap(send, "dp", 1)))
    awaited = ()
    for head, (kept, near) in enumerate(weight_parts):
        (send,) = call(
            add_near,
            [((2 * part_rows, 2 * HEAD_DIM), BF16)],
            (kept, near, *awaited),
            held=len(awaited),
            flops=0 if head else 2000000000,
        )
        awaited = (send,)
        weight_parts[head] = (kept, near, swap(send, "dp", 2))

    def pack(grad0, grad1, other0, other1, send, kept):
        _, spot, _ = place()
        for head, (grad, other) in enumerate(((grad0, other0), (grad1, other1))):
            padded = jnp.concatenate([grad[...], jnp.zeros((seq_len - seen, 2 * HEAD_DIM), BF16)], axis=0)
            for ref, wanted in ((kept, spot), (send, jnp.bitwise_xor(spot, 1))):
                chosen = jnp.zeros((tokens, 2 * HEAD_DIM), BF16)
                for block in range(4):
                    chosen = jnp.where(wanted == block, padded[block * tokens : (block + 1) * tokens], chosen)
                ref[:, head * 2 * HEAD_DIM : (head + 1) * 2 * HEAD_DIM] = chosen
            send[:, 2 * kv_width + head * group_width : 2 * kv_width + (head + 1) * group_width] = other[...]

    send, kept = call(
        pack,
        [((tokens, 2 * kv_width + width), BF16), ((tokens, 2 * kv_width), BF16)],
        (*grads, query_parts[0][1], query_parts[1][1]),
    )
    got = swap(send, "seq", 1)

    def unpack(kept_ref, got_ref, mine0, mine1, query_out, key_out, value_out):
        core, _, _ = place()
        for head, mine in enumerate((mine0, mine1)):
            query_out[:, lanes(core * width + head * group_width, group_width)] = mine[...]
            first = 2 * kv_width + head * group_width
            query_out[:, lanes((1 - core) * width + head * group_width, group_width)] = got_ref[:, first : first + group_width]
            for ref, side in ((kept_ref, core), (got_ref, 1 - core)):
                spot = lanes(side * kv_width + head * HEAD_DIM, HEAD_DIM)
                first = head * 2 * HEAD_DIM
                key_out[:, spot] = ref[:, first : first + HEAD_DIM]
                value_out[:, spot] = ref[:, first + HEAD_DIM : first + 2 * HEAD_DIM]

    query_grad, key_grad, value_grad = call(
        unpack,
        [((tokens, 2 * width), BF16), ((tokens, 2 * kv_width), BF16), ((tokens, 2 * kv_width), BF16)],
        (kept, got, query_parts[0][0], query_parts[1][0]),
    )

    def add_planes(kept, near, far, kept_out, send_out):
        core, _, _ = place()
        for out, owner in ((kept_out, core), (send_out, 1 - core)):
            rows = pl.ds(pl.multiple_of(owner * part_rows, part_rows), part_rows)
            out[...] = kept[rows, :] + (near[rows, :].astype(F32) + far[rows, :].astype(F32))

    pieces = []
    for parts in weight_parts:
        kept_weight, send_weight = call(add_planes, [((part_rows, 2 * HEAD_DIM), F32)] * 2, parts)
        pieces += [kept_weight, swap(send_weight, "seq", 1)]

    def join(kept0, got0, kept1, got1, out):
        core, _, _ = place()
        for head, (kept_ref, got_ref) in enumerate(((kept0, got0), (kept1, got1))):
            for ref, side in ((kept_ref, core), (got_ref, 1 - core)):
                spot = side * kv_width + head * HEAD_DIM
                out[:, lanes(spot, HEAD_DIM)] = ref[:, :HEAD_DIM]
                out[:, lanes(2 * kv_width + spot, HEAD_DIM)] = ref[:, HEAD_DIM:]

    (weight_grad,) = call(join, [((part_rows, 4 * kv_width), F32)], pieces)
    return query_grad[None], key_grad[None], value_grad[None], weight_grad


def solution(mesh):
    in_specs = (
        P("dp", "seq", None),
        P("dp", "seq", None),
        P("dp", "seq", None),
        P("dp", "seq", None),
        P("dp", "seq", None),
        P("dp"),
        P("dp"),
    )
    out_specs = (
        P("dp", "seq", None),
        P("dp", "seq", None),
        P("dp", "seq", None),
        P(("seq", "dp"), None),
    )
    body = local_pairs if (mesh.shape["seq"], mesh.shape["dp"]) == (2 * KV_HEADS, 4) else local
    return jax.shard_map(body, mesh=mesh, in_specs=in_specs, out_specs=out_specs, check_vma=False)
```
